32 devices in a mesh: groups: 2 (over x), spatial: 16 (over z, y, core).
Axes of the slice: x: 2, y: 2, z: 4, core: 2. Of those that a mesh axis runs over, the one named last changes fastest.
Arguments:
- volume: bfloat16 [32, 64, 8, 256], P(None, 'spatial', 'groups'), parts along dimension 2, may hold values from -6 to 6
- weights_mid: bfloat16 [64, 27, 32], replicated, may hold values from -0.21875 to 0.21875
- weights_top: bfloat16 [128, 27, 64], replicated, may hold values from -0.15625 to 0.15625
- cotangent: bfloat16 [128, 32, 4, 128], P(None, 'spatial', 'groups'), parts along dimension 2, may hold values from -6 to 6
Outputs:
- input_grad: bfloat16 [32, 64, 8, 256], P(None, 'spatial', 'groups'), parts along dimension 2
- mid_grad: float32 [128, 27, 32], P('groups'), parts along dimension 0
- top_grad: float32 [256, 27, 64], P('groups'), parts along dimension 0
The draws below stay inside these ranges and needn't reach their ends.
There are 2 independent parts, one for each index of `groups`. The reference program is written for one: setup_inputs(seed, part) draws one part's arguments, and reference() takes and returns one part's arrays. A program takes and returns all parts, laid end to end along the dimension named above; an argument that names none is the same for every part. Nothing has to cross between parts.
All inputs are finite; a program needn't handle non-finite values.
Results may differ from the reference program's by a relative error of at most 0.0059.
Values may be sent and summed in bfloat16 or wider, within the bound.
No kernel may reach another device: no remote copies, remote signals or barrier semaphores. Data moves between devices by JAX's collectives and lax.ppermute only.
A program may use at most 128 MiB of HBM per device.

```python
import math
import jax
import jax.numpy as jnp
from jax import lax

CIN = 32
CMID = 64
COUT = 128
H = 4
W = 256
NZ = 64
NZP = 32
HP = 2
WP = 128


def levels(stream_key, shape, cuts, smallest, high):
    level = 1.0
    for position, parts in cuts:
        steps = jax.random.uniform(jax.random.fold_in(jax.random.fold_in(stream_key, 6), position), (parts,), jnp.float32, smallest / len(cuts), high / len(cuts))
        level = level * jnp.repeat(jnp.exp(steps), shape[position] // parts).reshape((-1,) + (1,) * (len(shape) - 1 - position))
    return level


def centred(key, shape, deviation, limit, shards=(), held_as=jnp.bfloat16):
    result = jax.random.normal(key, shape, jnp.float32) * deviation
    if len(shards) > 0:
        result = levels(key, shape, shards, -0.22, 0.18) * result
    return jnp.clip(result, min=-limit, max=limit).astype(held_as)


def setup_inputs(seed: int = 0, part: int = 0) -> dict:
    seeds = jax.random.split(jax.random.key(seed), 5)
    part_keys = jax.random.split(jax.random.fold_in(seeds[4], part), 5)
    return {
        "volume": centred(part_keys[0], (CIN, NZ, H, W), 1.0, 6.0, ((1, 16),)),
        "weights_mid": centred(seeds[1], (CMID, 27, CIN), (27 * CIN) ** -0.5, 0.21875),
        "weights_top": centred(seeds[2], (COUT, 27, CMID), (27 * CMID) ** -0.5, 0.15625),
        "cotangent": centred(part_keys[3], (COUT, NZP, HP, WP), 1.0, 6.0, ((1, 16),)),
    }


def activate(values):
    return jax.nn.gelu(values, approximate=True)

def through(pre_values, incoming):
    return jax.vjp(activate, pre_values)[1](incoming)[0]

def offsets():
    return [(offset_z, offset_y, offset_x) for offset_z in (-1, 0, 1) for offset_y in (-1, 0, 1) for offset_x in (-1, 0, 1)]

def window(padded, offset, extent, orient):
    anchor_z = 1 + orient * offset[0]
    anchor_y = 1 + orient * offset[1]
    anchor_x = 1 + orient * offset[2]
    return padded[:, anchor_z:anchor_z + extent[0], anchor_y:anchor_y + extent[1], anchor_x:anchor_x + extent[2]]

def border(field):
    return jnp.pad(field, ((0, 0), (1, 1), (1, 1), (1, 1)))

def coarsen(field):
    shaped = field.reshape(field.shape[0], field.shape[1] // 2, 2, field.shape[2] // 2, 2, field.shape[3] // 2, 2)
    return lax.optimization_barrier(jnp.mean(shaped, axis=(2, 4, 6)))

def refine(field):
    return jnp.repeat(jnp.repeat(jnp.repeat(field, 2, axis=1), 2, axis=2), 2, axis=3)

def convolve(field, weights):
    padded = border(field)
    extent = field.shape[1:]
    running = jnp.zeros((weights.shape[0], field[0].size), jnp.float32)
    for number, offset in enumerate(offsets()):
        piece = window(padded, offset, extent, 1).reshape(field.shape[0], -1)
        running = running + jnp.dot(weights[:, number, :], piece, preferred_element_type=jnp.float32)
    return running.reshape((weights.shape[0],) + extent)

def transpose_conv(delta, weights):
    padded = border(delta)
    extent = delta.shape[1:]
    running = jnp.zeros((weights.shape[2], delta[0].size), jnp.float32)
    for number, offset in enumerate(offsets()):
        piece = window(padded, offset, extent, -1).reshape(delta.shape[0], -1)
        running = running + lax.dot_general(weights[:, number, :], piece, (((0,), (0,)), ((), ())), preferred_element_type=jnp.float32)
    return running.reshape((weights.shape[2],) + extent)

def weight_grad(delta, field):
    padded = border(field)
    extent = field.shape[1:]
    flat_delta = delta.reshape(delta.shape[0], -1)
    rows_list = []
    for offset in offsets():
        piece = window(padded, offset, extent, 1).reshape(field.shape[0], -1)
        rows_list.append(lax.dot_general(flat_delta, piece, (((1,), (1,)), ((), ())), preferred_element_type=jnp.float32))
    return jnp.stack(rows_list, axis=1)

def reference(volume, weights_mid, weights_top, cotangent):
    pre_mid = convolve(volume, weights_mid)
    pooled = coarsen(activate(pre_mid)).astype(jnp.bfloat16)
    pre_top = convolve(pooled, weights_top)
    delta_top = through(pre_top, cotangent.astype(jnp.float32)).astype(jnp.bfloat16)
    scale_top = 1.0 / math.sqrt(pooled[0].size)
    top_grad = weight_grad(delta_top, pooled) * scale_top
    grad_pool = transpose_conv(delta_top, weights_top)
    delta_mid = through(pre_mid, refine(grad_pool) * 0.125).astype(jnp.bfloat16)
    scale_mid = 1.0 / math.sqrt(volume[0].size)
    mid_grad = weight_grad(delta_mid, volume) * scale_mid
    input_grad = transpose_conv(delta_mid, weights_mid).astype(jnp.bfloat16)
    return (input_grad, mid_grad, top_grad)
```

```python
import math

import jax
import jax.numpy as jnp
from jax import lax
from jax.experimental import pallas as pl
from jax.experimental.pallas import tpu as pltpu
from jax.sharding import PartitionSpec as P

BF16 = jnp.bfloat16
F32 = jnp.float32
ROOT = math.sqrt(2.0 / math.pi)
CUBIC = 0.044715
THREE = (0, 1, 2)
VMEM_LIMIT = 50 << 20


def kernel_call(body, name, outs, args, scratch=(), flops=0, moved=0):
    whole = pl.BlockSpec(memory_space=pltpu.VMEM)
    return pl.pallas_call(
        body,
        name=name,
        out_shape=outs,
        in_specs=[whole] * len(args),
        out_specs=jax.tree.map(lambda _: whole, outs),
        scratch_shapes=list(scratch),
        compiler_params=pltpu.CompilerParams(vmem_limit_bytes=VMEM_LIMIT),
        cost_estimate=pl.CostEstimate(flops=flops, bytes_accessed=moved, transcendentals=0),
    )(*args)


def dot(a, b, contract=((1,), (0,))):
    return lax.dot_general(a, b, (contract, ((), ())), preferred_element_type=F32)


def parity_matrix(width, inverse):
    first = lax.broadcasted_iota(jnp.int32, (width, width), 0)
    second = lax.broadcasted_iota(jnp.int32, (width, width), 1)
    cell, slot = (second, first) if inverse else (first, second)
    half = width // 2
    source = jnp.where(slot < half, 2 * slot, 2 * (slot - half) + 1)
    return (cell == source).astype(F32).astype(BF16)


def later(row):
    lane = lax.broadcasted_iota(jnp.int32, row.shape, 1)
    return jnp.where(lane == 0, 0.0, pltpu.roll(row, 1, 1))


def earlier(row):
    lane = lax.broadcasted_iota(jnp.int32, row.shape, 1)
    last = row.shape[1] - 1
    return jnp.where(lane == last, 0.0, pltpu.roll(row, last, 1))


def gelu_parts(value):
    square = value * value
    tanh = jnp.tanh(ROOT * value * (1.0 + CUBIC * square))
    outer = 0.5 * (1.0 + tanh)
    slope = outer + 0.5 * value * (1.0 - tanh * tanh) * (ROOT * (1.0 + 3.0 * CUBIC * square))
    return value * outer, slope


def forward_kernel(prev_ref, own_ref, next_ref, wmid_ref, wtop_ref, cot_ref, delta_ref, slope_ref, vol_ref, pool_ref, *, h, w, spatial):
    half = w // 2
    here = lax.axis_index("spatial")
    split = parity_matrix(w, False)
    vrows = h + 2
    zero_row = jnp.zeros((vol_ref.shape[0], w), BF16)
    planes = []
    for ref in (prev_ref, own_ref, next_ref):
        for start in range(0, ref.shape[1], h * w):
            planes.append((ref, start))
    channels = vol_ref.shape[0]
    for z, (ref, start) in enumerate(planes):
        rows = jnp.concatenate([ref[:, start + y * w : start + (y + 1) * w] for y in range(h)], axis=0)
        sorted_rows = dot(rows, split).astype(BF16)
        base = z * vrows * w
        vol_ref[:, base : base + w] = zero_row
        vol_ref[:, base + (h + 1) * w : base + (h + 2) * w] = zero_row
        for y in range(h):
            vol_ref[:, base + (y + 1) * w : base + (y + 2) * w] = sorted_rows[y * channels : (y + 1) * channels]
    mid = slope_ref.shape[0]
    count = len(planes) - 2
    hp = h // 2
    prow = (hp + 2) * half
    pool_zero = jnp.zeros((pool_ref.shape[0], half), BF16)
    for pz in range(count // 2):
        sums = [None] * hp
        for j in (2 * pz, 2 * pz + 1):
            cols = jnp.concatenate(
                [vol_ref[:, ((j + a) * vrows + b) * w : ((j + a) * vrows + b + h) * w] for a in THREE for b in THREE],
                axis=0,
            )
            part = dot(wmid_ref[...], cols)
            for y in range(h):
                even = slice(y * w, y * w + half)
                odd = slice(y * w + half, (y + 1) * w)
                pre_even = part[mid : 2 * mid, even] + later(part[:mid, odd]) + part[2 * mid :, odd]
                pre_odd = part[mid : 2 * mid, odd] + part[:mid, even] + earlier(part[2 * mid :, even])
                value_even, slope_even = gelu_parts(pre_even)
                value_odd, slope_odd = gelu_parts(pre_odd)
                if 0 < j < count - 1:
                    out = ((j - 1) * h + y) * w
                    slope_ref[:, out : out + half] = slope_even * 0.125
                    slope_ref[:, out + half : out + w] = slope_odd * 0.125
                both = value_even + value_odd
                sums[y // 2] = both if sums[y // 2] is None else sums[y // 2] + both
        base = pz * prow
        pool_ref[:, base : base + half] = pool_zero
        pool_ref[:, base + (hp + 1) * half : base + prow] = pool_zero
        for y in range(hp):
            row = sums[y] * 0.125
            if pz == 0:
                row = jnp.where(here == 0, 0.0, row)
            if pz == count // 2 - 1:
                row = jnp.where(here == spatial - 1, 0.0, row)
            row = row.astype(BF16).astype(F32)
            at = slice(base + (y + 1) * half, base + (y + 2) * half)
            pool_ref[:mid, at] = later(row).astype(BF16)
            pool_ref[mid : 2 * mid, at] = row.astype(BF16)
            pool_ref[2 * mid :, at] = earlier(row).astype(BF16)
    for j in range(count // 2 - 2):
        cols = jnp.concatenate(
            [pool_ref[:, (j + a) * prow + b * half : (j + a) * prow + (b + hp) * half] for a in THREE for b in THREE], axis=0
        )
        pre_top = dot(wtop_ref[...], cols, ((0,), (0,)))
        at = slice(j * hp * half, (j + 1) * hp * half)
        delta_ref[:, at] = (cot_ref[:, at].astype(F32) * gelu_parts(pre_top)[1]).astype(BF16)


def top_kernel(delta_ref, pool_ref, out_ref, *, hp, wp):
    prow = (hp + 2) * wp
    planes = delta_ref.shape[1] // (hp * wp)
    for a in THREE:
        for b in THREE:
            block = jnp.concatenate(
                [pool_ref[:, (j + a) * prow + b * wp : (j + a) * prow + (b + hp) * wp] for j in range(planes)], axis=1
            )
            rows = slice((3 * a + b) * block.shape[0], (3 * a + b + 1) * block.shape[0])
            out_ref[rows, :] = dot(block, delta_ref[...], ((1,), (1,))).astype(BF16)


def backward_kernel(prev_ref, own_ref, next_ref, slope_ref, vol_ref, wtop_ref, mid_ref, field_ref, top_ref, shift_ref, *, h, w, spatial):
    half, hp = w // 2, h // 2
    here = lax.axis_index("spatial")
    trow = (hp + 2) * half
    top_zero = jnp.zeros((top_ref.shape[0], half), BF16)
    depth = own_ref.shape[1] // (hp * half)
    for z in range(3 * depth):
        ref = (prev_ref, own_ref, next_ref)[z // depth]
        start = (z % depth) * hp * half
        base = z * trow
        top_ref[:, base : base + half] = top_zero
        top_ref[:, base + half : base + (hp + 1) * half] = ref[:, start : start + hp * half]
        top_ref[:, base + (hp + 1) * half : base + trow] = top_zero
    mid = slope_ref.shape[0]
    weights = jnp.concatenate(
        [
            jnp.concatenate([wtop_ref[(3 * ab + c) * mid : (3 * ab + c + 1) * mid, :] for ab in range(9)], axis=1)
            for c in THREE
        ],
        axis=0,
    )
    outer = depth + 2
    first = depth - 1
    cols = jnp.concatenate(
        [
            jnp.concatenate(
                [
                    top_ref[:, (first + j + 1 - a) * trow + (2 - b) * half : (first + j + 1 - a) * trow + (2 - b + hp) * half]
                    for j in range(outer)
                ],
                axis=1,
            )
            for a in THREE
            for b in THREE
        ],
        axis=0,
    )
    part = dot(weights, cols)
    vrows = h + 2
    field_zero = jnp.zeros((mid, w), BF16)
    fine = 2 * depth
    for m in range(fine + 2):
        j = (m + 1) // 2
        base = m * vrows * w
        field_ref[:, base : base + w] = field_zero
        field_ref[:, base + (h + 1) * w : base + vrows * w] = field_zero
        for y in range(h):
            at = slice((j * hp + y // 2) * half, (j * hp + y // 2 + 1) * half)
            pool = part[mid : 2 * mid, at] + later(part[2 * mid :, at]) + earlier(part[:mid, at])
            if m == 0:
                pool = jnp.where(here == 0, 0.0, pool)
            if m == fine + 1:
                pool = jnp.where(here == spatial - 1, 0.0, pool)
            out = (m * h + y) * w
            even = (slope_ref[:, out : out + half] * pool).astype(BF16)
            odd = (slope_ref[:, out + half : out + w] * pool).astype(BF16)
            to = base + (y + 1) * w
            field_ref[:, to : to + half] = even
            field_ref[:, to + half : to + w] = odd
            if 0 < m <= fine:
                to = ((m - 1) * h + y) * w
                shift_ref[:mid, to : to + half] = odd
                shift_ref[:mid, to + half : to + w] = earlier(even.astype(F32)).astype(BF16)
                shift_ref[mid : 2 * mid, to : to + half] = even
                shift_ref[mid : 2 * mid, to + half : to + w] = odd
                shift_ref[2 * mid :, to : to + half] = later(odd.astype(F32)).astype(BF16)
                shift_ref[2 * mid :, to + half : to + w] = even
    total = None
    for z in range(fine):
        piece = jnp.concatenate(
            [
                vol_ref[:, ((z + 2 + a) * vrows + b) * w : ((z + 2 + a) * vrows + b + h) * w]
                for a in THREE
                for b in THREE
            ],
            axis=0,
        )
        product = dot(piece, shift_ref[:, z * h * w : (z + 1) * h * w], ((1,), (1,)))
        total = product if total is None else total + product
    rows = total.shape[0]
    mid_ref[:rows, :] = total[:, : 2 * mid].astype(BF16)
    mid_ref[rows:, :] = jnp.concatenate([total[:, 2 * mid :], jnp.zeros((rows, mid), F32)], axis=1).astype(BF16)


def input_kernel(field_ref, wback_ref, out_ref, *, h, w):
    half = w // 2
    vrows = h + 2
    join = parity_matrix(w, True)
    ch = out_ref.shape[0]
    for z in range(out_ref.shape[1] // (h * w)):
        cols = jnp.concatenate(
            [
                field_ref[:, ((z + 2 - a) * vrows + 2 - b) * w : ((z + 2 - a) * vrows + 2 - b + h) * w]
                for a in THREE
                for b in THREE
            ],
            axis=0,
        )
        part = dot(wback_ref[...], cols)
        rows = []
        for y in range(h):
            even = slice(y * w, y * w + half)
            odd = slice(y * w + half, (y + 1) * w)
            grad_even = part[ch : 2 * ch, even] + later(part[2 * ch :, odd]) + part[:ch, odd]
            grad_odd = part[ch : 2 * ch, odd] + part[2 * ch :, even] + earlier(part[:ch, even])
            rows.append(jnp.concatenate([grad_even, grad_odd], axis=1).astype(BF16))
        joined = dot(jnp.concatenate(rows, axis=0), join).astype(BF16)
        for y in range(h):
            out_ref[:, (z * h + y) * w : (z * h + y + 1) * w] = joined[y * ch : (y + 1) * ch]


def finish_kernel(sum_ref, top_ref, mid_ref, *, scale_top, scale_mid):
    top_rows = top_ref.shape[0]
    top_ref[...] = sum_ref[:top_rows].astype(F32) * scale_top
    rows = mid_ref.shape[0] // 3
    mid = mid_ref.shape[1]
    left = sum_ref[top_rows : top_rows + rows].astype(F32) * scale_mid
    right = sum_ref[top_rows + rows :].astype(F32) * scale_mid
    q = rows // 9
    for ab in range(9):
        block = slice(ab * q, (ab + 1) * q)
        mid_ref[(3 * ab) * q : (3 * ab + 1) * q, :] = left[block, :mid]
        mid_ref[(3 * ab + 1) * q : (3 * ab + 2) * q, :] = left[block, mid:]
        mid_ref[(3 * ab + 2) * q : (3 * ab + 3) * q, :] = right[block, :mid]


def neighbours(shard, upward):
    size = lax.axis_size("spatial")
    pairs = [(i, i + 1) if upward else (i + 1, i) for i in range(size - 1)]
    return lax.ppermute(shard, "spatial", pairs)


def partner(block, bit):
    size = lax.axis_size("spatial")
    return lax.ppermute(block, "spatial", [(i, i ^ bit) for i in range(size)])


def sum_over_slabs(block, halvings):
    here = lax.axis_index("spatial")
    bits = [1 << k for k in range(lax.axis_size("spatial").bit_length() - 1)]
    kept = []
    for number, bit in enumerate(bits):
        if number < halvings:
            rows = block.shape[0] // 2
            low = (here // bit) % 2 == 0
            mine = jnp.where(low, block[:rows], block[rows:])
            other = jnp.where(low, block[rows:], block[:rows])
            block = mine + partner(other, bit)
            kept.append((bit, low))
        else:
            block = block + partner(block, bit)
    for bit, low in reversed(kept):
        other = partner(block, bit)
        block = jnp.where(low, jnp.concatenate([block, other]), jnp.concatenate([other, block]))
    return block


def shards(volume, weights_mid, weights_top, cotangent):
    spatial = lax.axis_size("spatial")
    cin, nz, h, w = volume.shape
    mid = weights_mid.shape[0]
    cout, nzp, hp, wp = cotangent.shape
    shape = jax.ShapeDtypeStruct
    plane = h * w
    flat = volume.reshape(cin, nz * plane)
    prev = neighbours(flat[:, plane:], True)
    following = neighbours(flat[:, : (nz - 1) * plane], False)
    split = weights_mid.reshape(mid, 9, 3, cin)
    wmid = jnp.transpose(split, (2, 0, 1, 3)).reshape(3 * mid, 9 * cin)
    wback = jnp.transpose(split, (2, 3, 1, 0)).reshape(3 * cin, 9 * mid)
    wtop = jnp.transpose(weights_top, (1, 2, 0)).reshape(27 * mid, cout)
    cot = cotangent.reshape(cout, nzp * hp * wp)
    padded = (3 * nz - 2) * (h + 2) * w
    delta, slope, vol, pool = kernel_call(
        lambda *refs: forward_kernel(*refs, h=h, w=w, spatial=spatial),
        "forward",
        (
            shape(cot.shape, BF16),
            shape((mid, (nz + 2) * plane), F32),
            shape((cin, padded), BF16),
            shape((3 * mid, (nzp + 2) * (hp + 2) * wp), BF16),
        ),
        (prev, flat, following, wmid, wtop, cot),
        flops=1_200_000_000,
        moved=6_000_000,
    )
    delta_prev = neighbours(delta, True)
    delta_next = neighbours(delta, False)
    top_part = kernel_call(
        lambda *refs: top_kernel(*refs, hp=hp, wp=wp),
        "top_part",
        shape((27 * mid, cout), BF16),
        (delta, pool),
        flops=226_000_000,
        moved=1_500_000,
    )
    mid_part, field = kernel_call(
        lambda *refs: backward_kernel(*refs, h=h, w=w, spatial=spatial),
        "backward",
        (shape((18 * cin, 2 * mid), BF16), shape((mid, (nz + 2) * (h + 2) * w), BF16)),
        (delta_prev, delta, delta_next, slope, vol, wtop),
        scratch=(pltpu.VMEM((cout, 3 * nzp * (hp + 2) * wp), BF16), pltpu.VMEM((3 * mid, nz * plane), BF16)),
        flops=900_000_000,
        moved=5_000_000,
    )
    total = sum_over_slabs(jnp.concatenate([top_part, mid_part], axis=0), 2)
    input_grad = kernel_call(
        lambda *refs: input_kernel(*refs, h=h, w=w),
        "input_grad",
        shape((cin, nz * plane), BF16),
        (field, wback),
        flops=452_000_000,
        moved=2_000_000,
    ).reshape(volume.shape)
    top_grad, mid_grad = kernel_call(
        lambda *refs: finish_kernel(
            *refs,
            scale_top=1.0 / math.sqrt(nzp * hp * wp * spatial),
            scale_mid=1.0 / math.sqrt(nz * plane * spatial),
        ),
        "finish",
        (shape((27 * mid, cout), F32), shape((27 * cin, mid), F32)),
        (total,),
        moved=2_000_000,
    )
    return (
        input_grad,
        jnp.transpose(mid_grad.reshape(27, cin, mid), (2, 0, 1)),
        jnp.transpose(top_grad.reshape(27, mid, cout), (2, 0, 1)),
    )


def solution(mesh):
    return jax.shard_map(
        shards,
        mesh=mesh,
        in_specs=(P(None, "spatial", "groups", None), P(), P(), P(None, "spatial", "groups", None)),
        out_specs=(
            P(None, "spatial", "groups", None),
            P("groups", None, None),
            P("groups", None, None),
        ),
        check_vma=False,
    )
```

```python
import math

import jax
import jax.numpy as jnp
from jax import lax
from jax.experimental import pallas as pl
from jax.experimental.pallas import tpu as pltpu
from jax.sharding import PartitionSpec as P

BF16 = jnp.bfloat16
F32 = jnp.float32
ROOT = math.sqrt(2.0 / math.pi)
CUBIC = 0.044715
THREE = (0, 1, 2)
VMEM_LIMIT = 50 << 20


def kernel_call(body, name, outs, args, scratch=(), flops=0, moved=0):
    whole = pl.BlockSpec(memory_space=pltpu.VMEM)
    return pl.pallas_call(
        body,
        name=name,
        out_shape=outs,
        in_specs=[whole] * len(args),
        out_specs=jax.tree.map(lambda _: whole, outs),
        scratch_shapes=list(scratch),
        compiler_params=pltpu.CompilerParams(vmem_limit_bytes=VMEM_LIMIT),
        cost_estimate=pl.CostEstimate(flops=flops, bytes_accessed=moved, transcendentals=0),
    )(*args)


def dot(a, b, contract=((1,), (0,))):
    return lax.dot_general(a, b, (contract, ((), ())), preferred_element_type=F32)


def parity_matrix(width, inverse):
    first = lax.broadcasted_iota(jnp.int32, (width, width), 0)
    second = lax.broadcasted_iota(jnp.int32, (width, width), 1)
    cell, slot = (second, first) if inverse else (first, second)
    half = width // 2
    source = jnp.where(slot < half, 2 * slot, 2 * (slot - half) + 1)
    return (cell == source).astype(F32).astype(BF16)


def later(row):
    lane = lax.broadcasted_iota(jnp.int32, row.shape, 1)
    return jnp.where(lane == 0, 0.0, pltpu.roll(row, 1, 1))


def earlier(row):
    lane = lax.broadcasted_iota(jnp.int32, row.shape, 1)
    last = row.shape[1] - 1
    return jnp.where(lane == last, 0.0, pltpu.roll(row, last, 1))


def gelu_parts(value):
    square = value * value
    tanh = jnp.tanh(ROOT * value * (1.0 + CUBIC * square))
    outer = 0.5 * (1.0 + tanh)
    slope = outer + 0.5 * value * (1.0 - tanh * tanh) * (ROOT * (1.0 + 3.0 * CUBIC * square))
    return value * outer, slope


def forward_kernel(near_ref, own_ref, far_ref, wmid_ref, wtop_ref, cot_ref, delta_ref, slope_ref, vol_ref, pool_ref, *, h, w, spatial):
    half = w // 2
    here = lax.axis_index("spatial")
    first = here % 2 == 0
    split = parity_matrix(w, False)
    vrows = h + 2
    zero_row = jnp.zeros((vol_ref.shape[0], w), BF16)
    planes = []
    for part, ref in enumerate((near_ref, own_ref, near_ref)):
        for start in range(0, ref.shape[1], h * w):
            planes.append((part, start))
    channels = vol_ref.shape[0]
    for z, (part, start) in enumerate(planes):
        rows = []
        for at in range(start, start + h * w, w):
            if part == 1:
                rows.append(own_ref[:, at : at + w])
            else:
                rows.append(jnp.where(first == (part == 0), far_ref[:, at : at + w], near_ref[:, at : at + w]))
        rows = jnp.concatenate(rows, axis=0)
        sorted_rows = dot(rows, split).astype(BF16)
        base = z * vrows * w
        vol_ref[:, base : base + w] = zero_row
        vol_ref[:, base + (h + 1) * w : base + (h + 2) * w] = zero_row
        for y in range(h):
            vol_ref[:, base + (y + 1) * w : base + (y + 2) * w] = sorted_rows[y * channels : (y + 1) * channels]
    mid = slope_ref.shape[0]
    count = len(planes) - 2
    hp = h // 2
    prow = (hp + 2) * half
    pool_zero = jnp.zeros((pool_ref.shape[0], half), BF16)
    for pz in range(count // 2):
        sums = [None] * hp
        for j in (2 * pz, 2 * pz + 1):
            cols = jnp.concatenate(
                [vol_ref[:, ((j + a) * vrows + b) * w : ((j + a) * vrows + b + h) * w] for a in THREE for b in THREE],
                axis=0,
            )
            part = dot(wmid_ref[...], cols)
            for y in range(h):
                even = slice(y * w, y * w + half)
                odd = slice(y * w + half, (y + 1) * w)
                pre_even = part[mid : 2 * mid, even] + later(part[:mid, odd]) + part[2 * mid :, odd]
                pre_odd = part[mid : 2 * mid, odd] + part[:mid, even] + earlier(part[2 * mid :, even])
                value_even, slope_even = gelu_parts(pre_even)
                value_odd, slope_odd = gelu_parts(pre_odd)
                if 0 < j < count - 1:
                    out = ((j - 1) * h + y) * w
                    slope_ref[:, out : out + half] = slope_even * 0.125
                    slope_ref[:, out + half : out + w] = slope_odd * 0.125
                both = value_even + value_odd
                sums[y // 2] = both if sums[y // 2] is None else sums[y // 2] + both
        base = pz * prow
        pool_ref[:, base : base + half] = pool_zero
        pool_ref[:, base + (hp + 1) * half : base + prow] = pool_zero
        for y in range(hp):
            row = sums[y] * 0.125
            if pz == 0:
                row = jnp.where(here == 0, 0.0, row)
            if pz == count // 2 - 1:
                row = jnp.where(here == spatial - 1, 0.0, row)
            row = row.astype(BF16).astype(F32)
            at = slice(base + (y + 1) * half, base + (y + 2) * half)
            pool_ref[:mid, at] = later(row).astype(BF16)
            pool_ref[mid : 2 * mid, at] = row.astype(BF16)
            pool_ref[2 * mid :, at] = earlier(row).astype(BF16)
    for j in range(count // 2 - 2):
        cols = jnp.concatenate(
            [pool_ref[:, (j + a) * prow + b * half : (j + a) * prow + (b + hp) * half] for a in THREE for b in THREE], axis=0
        )
        pre_top = dot(wtop_ref[...], cols, ((0,), (0,)))
        at = slice(j * hp * half, (j + 1) * hp * half)
        delta_ref[:, at] = (cot_ref[:, at].astype(F32) * gelu_parts(pre_top)[1]).astype(BF16)


def halve(whole_ref, keep_ref, send_ref):
    core = lax.axis_index("spatial") % 2
    rows = keep_ref.shape[0]
    keep_ref[...] = whole_ref[pl.ds(pl.multiple_of(core * rows, 16), rows), :]
    send_ref[...] = whole_ref[pl.ds(pl.multiple_of((1 - core) * rows, 16), rows), :].astype(BF16)


def top_kernel(delta_ref, pool_ref, keep_ref, send_ref, out_ref, *, hp, wp):
    prow = (hp + 2) * wp
    planes = delta_ref.shape[1] // (hp * wp)
    for a in THREE:
        for b in THREE:
            block = jnp.concatenate(
                [pool_ref[:, (j + a) * prow + b * wp : (j + a) * prow + (b + hp) * wp] for j in range(planes)], axis=1
            )
            rows = slice((3 * a + b) * block.shape[0], (3 * a + b + 1) * block.shape[0])
            out_ref[rows, :] = dot(block, delta_ref[...], ((1,), (1,)))
    halve(out_ref, keep_ref, send_ref)


def backward_kernel(
    near_ref, own_ref, far_ref, slope_ref, vol_ref, wtop_ref, keep_ref, send_ref, field_ref, top_ref, shift_ref, mid_ref, *, h, w, spatial
):
    half, hp = w // 2, h // 2
    here = lax.axis_index("spatial")
    trow = (hp + 2) * half
    top_zero = jnp.zeros((top_ref.shape[0], half), BF16)
    depth = own_ref.shape[1] // (hp * half)
    for z in range(3 * depth):
        start = (z % depth) * hp * half
        at = slice(start, start + hp * half)
        if z // depth == 1:
            plane = own_ref[:, at]
        else:
            plane = jnp.where((here % 2 == 0) == (z < depth), far_ref[:, at], near_ref[:, at])
        base = z * trow
        top_ref[:, base : base + half] = top_zero
        top_ref[:, base + half : base + (hp + 1) * half] = plane
        top_ref[:, base + (hp + 1) * half : base + trow] = top_zero
    mid = slope_ref.shape[0]
    weights = jnp.concatenate(
        [
            jnp.concatenate([wtop_ref[(3 * ab + c) * mid : (3 * ab + c + 1) * mid, :] for ab in range(9)], axis=1)
            for c in THREE
        ],
        axis=0,
    )
    outer = depth + 2
    first = depth - 1
    cols = jnp.concatenate(
        [
            jnp.concatenate(
                [
                    top_ref[:, (first + j + 1 - a) * trow + (2 - b) * half : (first + j + 1 - a) * trow + (2 - b + hp) * half]
                    for j in range(outer)
                ],
                axis=1,
            )
            for a in THREE
            for b in THREE
        ],
        axis=0,
    )
    part = dot(weights, cols)
    vrows = h + 2
    field_zero = jnp.zeros((mid, w), BF16)
    fine = 2 * depth
    for m in range(fine + 2):
        j = (m + 1) // 2
        base = m * vrows * w
        field_ref[:, base : base + w] = field_zero
        field_ref[:, base + (h + 1) * w : base + vrows * w] = field_zero
        for y in range(h):
            at = slice((j * hp + y // 2) * half, (j * hp + y // 2 + 1) * half)
            pool = part[mid : 2 * mid, at] + later(part[2 * mid :, at]) + earlier(part[:mid, at])
            if m == 0:
                pool = jnp.where(here == 0, 0.0, pool)
            if m == fine + 1:
                pool = jnp.where(here == spatial - 1, 0.0, pool)
            out = (m * h + y) * w
            even = (slope_ref[:, out : out + half] * pool).astype(BF16)
            odd = (slope_ref[:, out + half : out + w] * pool).astype(BF16)
            to = base + (y + 1) * w
            field_ref[:, to : to + half] = even
            field_ref[:, to + half : to + w] = odd
            if 0 < m <= fine:
                to = ((m - 1) * h + y) * w
                shift_ref[:mid, to : to + half] = odd
                shift_ref[:mid, to + half : to + w] = earlier(even.astype(F32)).astype(BF16)
                shift_ref[mid : 2 * mid, to : to + half] = even
                shift_ref[mid : 2 * mid, to + half : to + w] = odd
                shift_ref[2 * mid :, to : to + half] = later(odd.astype(F32)).astype(BF16)
                shift_ref[2 * mid :, to + half : to + w] = even
    total = None
    for z in range(fine):
        piece = jnp.concatenate(
            [
                vol_ref[:, ((z + 2 + a) * vrows + b) * w : ((z + 2 + a) * vrows + b + h) * w]
                for a in THREE
                for b in THREE
            ],
            axis=0,
        )
        product = dot(piece, shift_ref[:, z * h * w : (z + 1) * h * w], ((1,), (1,)))
        total = product if total is None else total + product
    rows = total.shape[0]
    half_rows = rows // 2
    mid_ref[:rows, :] = total[:, : 2 * mid]
    last = total[:, 2 * mid :]
    mid_ref[rows : rows + half_rows, :] = jnp.concatenate([last[:half_rows], last[half_rows:]], axis=1)
    spare = mid_ref.shape[0] - rows - half_rows
    if spare:
        mid_ref[rows + half_rows :, :] = jnp.zeros((spare, 2 * mid), F32)
    halve(mid_ref, keep_ref, send_ref)


def input_kernel(field_ref, wback_ref, out_ref, *, h, w):
    half = w // 2
    vrows = h + 2
    join = parity_matrix(w, True)
    ch = out_ref.shape[0]
    for z in range(out_ref.shape[1] // (h * w)):
        cols = jnp.concatenate(
            [
                field_ref[:, ((z + 2 - a) * vrows + 2 - b) * w : ((z + 2 - a) * vrows + 2 - b + h) * w]
                for a in THREE
                for b in THREE
            ],
            axis=0,
        )
        part = dot(wback_ref[...], cols)
        rows = []
        for y in range(h):
            even = slice(y * w, y * w + half)
            odd = slice(y * w + half, (y + 1) * w)
            grad_even = part[ch : 2 * ch, even] + later(part[2 * ch :, odd]) + part[:ch, odd]
            grad_odd = part[ch : 2 * ch, odd] + part[2 * ch :, even] + earlier(part[:ch, even])
            rows.append(jnp.concatenate([grad_even, grad_odd], axis=1).astype(BF16))
        joined = dot(jnp.concatenate(rows, axis=0), join).astype(BF16)
        for y in range(h):
            out_ref[:, (z * h + y) * w : (z * h + y + 1) * w] = joined[y * ch : (y + 1) * ch]


def finish_kernel(low_ref, high_ref, out_ref, *, scale):
    rows = out_ref.shape[0] // 3
    mid = out_ref.shape[1]
    whole = jnp.concatenate([low_ref[...], high_ref[...]], axis=0) * scale
    q = rows // 9
    for ab in range(9):
        block = whole[ab * q : (ab + 1) * q]
        out_ref[(3 * ab) * q : (3 * ab + 1) * q, :] = block[:, :mid]
        out_ref[(3 * ab + 1) * q : (3 * ab + 2) * q, :] = block[:, mid:]
    half_rows = rows // 2
    last = whole[rows : rows + half_rows]
    last = jnp.concatenate([last[:, :mid], last[:, mid:]], axis=0)
    for ab in range(9):
        out_ref[(3 * ab + 2) * q : (3 * ab + 3) * q, :] = last[ab * q : (ab + 1) * q]


def partner(block, bit):
    size = lax.axis_size("spatial")
    return lax.ppermute(block, "spatial", [(i, i ^ bit) for i in range(size)])


def across(block):
    size = lax.axis_size("spatial")
    pairs = [(i, i + 1) for i in range(1, size - 1, 2)]
    return lax.ppermute(block, "spatial", pairs + [(j, i) for i, j in pairs])


def bit_is_clear(bit):
    return (lax.axis_index("spatial") // bit) % 2 == 0


def add_both(block, bit):
    rounded = block.astype(BF16)
    return rounded.astype(F32) + partner(rounded, bit).astype(F32)


def halves(block, bit):
    rows = block.shape[0] // 2
    low = bit_is_clear(bit)
    mine = jnp.where(low, block[:rows], block[rows:])
    other = jnp.where(low, block[rows:], block[:rows])
    return mine, other.astype(BF16)


def in_order(block, other, bit):
    low = bit_is_clear(bit)
    return jnp.where(low, block, other), jnp.where(low, other, block)


def far_bits():
    return [1 << k for k in range(2, lax.axis_size("spatial").bit_length() - 1)]


def shards(volume, weights_mid, weights_top, cotangent):
    spatial = lax.axis_size("spatial")
    cin, nz, h, w = volume.shape
    mid = weights_mid.shape[0]
    cout, nzp, hp, wp = cotangent.shape
    shape = jax.ShapeDtypeStruct
    plane = h * w
    flat = volume.reshape(cin, nz * plane)
    early, late = flat[:, : (nz - 1) * plane], flat[:, plane:]
    first_core = bit_is_clear(1)
    far = across(jnp.where(first_core, early, late))
    near = partner(jnp.where(first_core, late, early), 1)
    split = weights_mid.reshape(mid, 9, 3, cin)
    wmid = jnp.transpose(split, (2, 0, 1, 3)).reshape(3 * mid, 9 * cin)
    wback = jnp.transpose(split, (2, 3, 1, 0)).reshape(3 * cin, 9 * mid)
    wtop = jnp.transpose(weights_top, (1, 2, 0)).reshape(27 * mid, cout)
    cot = cotangent.reshape(cout, nzp * hp * wp)
    padded = (3 * nz - 2) * (h + 2) * w
    delta, slope, vol, pool = kernel_call(
        lambda *refs: forward_kernel(*refs, h=h, w=w, spatial=spatial),
        "forward",
        (
            shape(cot.shape, BF16),
            shape((mid, (nz + 2) * plane), F32),
            shape((cin, padded), BF16),
            shape((3 * mid, (nzp + 2) * (hp + 2) * wp), BF16),
        ),
        (near, flat, far, wmid, wtop, cot),
        flops=1_200_000_000,
        moved=6_000_000,
    )
    delta_far = across(delta)
    delta_near = partner(delta, 1)
    top_rows = 27 * mid
    keep, send = kernel_call(
        lambda *refs: top_kernel(*refs, hp=hp, wp=wp),
        "top_part",
        (shape((top_rows // 2, cout), F32), shape((top_rows // 2, cout), BF16)),
        (delta, pool),
        scratch=(pltpu.VMEM((top_rows, cout), F32),),
        flops=226_000_000,
        moved=1_500_000,
    )
    top_sum = keep + partner(send, 1).astype(F32)
    mine, other = halves(top_sum, 2)
    other, delta_near, delta_far = lax.optimization_barrier((other, delta_near, delta_far))
    top_sum = mine + partner(other, 2).astype(F32)
    for bit in far_bits():
        top_sum = add_both(top_sum, bit)
    top_sum = top_sum.astype(BF16)
    top_sum = jnp.concatenate(in_order(top_sum, partner(top_sum, 2), 2), axis=0)
    top_sum = jnp.concatenate(in_order(top_sum, partner(top_sum, 1), 1), axis=0)
    top_grad = top_sum.astype(F32) * (1.0 / math.sqrt(nzp * hp * wp * spatial))
    mid_rows = -(-27 * cin // 64) * 16
    keep, send, field = kernel_call(
        lambda *refs: backward_kernel(*refs, h=h, w=w, spatial=spatial),
        "backward",
        (
            shape((mid_rows, 2 * mid), F32),
            shape((mid_rows, 2 * mid), BF16),
            shape((mid, (nz + 2) * (h + 2) * w), BF16),
        ),
        (delta_near, delta, delta_far, slope, vol, wtop),
        scratch=(
            pltpu.VMEM((cout, 3 * nzp * (hp + 2) * wp), BF16),
            pltpu.VMEM((3 * mid, nz * plane), BF16),
            pltpu.VMEM((2 * mid_rows, 2 * mid), F32),
        ),
        flops=900_000_000,
        moved=5_000_000,
    )
    mid_sum = keep + partner(send, 1).astype(F32)
    mid_sum, field = lax.optimization_barrier((mid_sum, field))
    for bit in [2] + far_bits():
        mid_sum = add_both(mid_sum, bit)
    mid_low, mid_high = in_order(mid_sum, partner(mid_sum, 1), 1)
    mid_grad = kernel_call(
        lambda *refs: finish_kernel(*refs, scale=1.0 / math.sqrt(nz * plane * spatial)),
        "finish",
        shape((27 * cin, mid), F32),
        (mid_low, mid_high),
        moved=1_000_000,
    )
    input_grad = kernel_call(
        lambda *refs: input_kernel(*refs, h=h, w=w),
        "input_grad",
        shape((cin, nz * plane), BF16),
        (field, wback),
        flops=452_000_000,
        moved=2_000_000,
    ).reshape(volume.shape)
    return (
        input_grad,
        jnp.transpose(mid_grad.reshape(27, cin, mid), (2, 0, 1)),
        jnp.transpose(top_grad.reshape(27, mid, cout), (2, 0, 1)),
    )


def solution(mesh):
    return jax.shard_map(
        shards,
        mesh=mesh,
        in_specs=(P(None, "spatial", "groups", None), P(), P(), P(None, "spatial", "groups", None)),
        out_specs=(
            P(None, "spatial", "groups", None),
            P("groups", None, None),
            P("groups", None, None),
        ),
        check_vma=False,
    )
```

```python
import math

import jax
import jax.numpy as jnp
from jax import lax
from jax.experimental import pallas as pl
from jax.experimental.pallas import tpu as pltpu
from jax.sharding import PartitionSpec as P

BF16 = jnp.bfloat16
F32 = jnp.float32
ROOT = math.sqrt(2.0 / math.pi)
CUBIC = 0.044715
THREE = (0, 1, 2)
VMEM_LIMIT = 20 << 20


def kernel_call(body, name, outs, args, scratch=(), flops=0, moved=0, last=False):
    whole = pl.BlockSpec(memory_space=pltpu.VMEM)
    args = [pltpu.with_memory_space_constraint(arg, pltpu.VMEM) for arg in args]
    if not last:
        outs = jax.tree.map(lambda out: pltpu.VMEM(out.shape, out.dtype), outs)
    return pl.pallas_call(
        body,
        name=name,
        out_shape=outs,
        in_specs=[whole] * len(args),
        out_specs=jax.tree.map(lambda _: whole, outs),
        scratch_shapes=list(scratch),
        compiler_params=pltpu.CompilerParams(vmem_limit_bytes=VMEM_LIMIT),
        cost_estimate=pl.CostEstimate(flops=flops, bytes_accessed=moved, transcendentals=0),
    )(*args)


def dot(a, b, contract=((1,), (0,))):
    return lax.dot_general(a, b, (contract, ((), ())), preferred_element_type=F32)


def parity_matrix(width, inverse):
    first = lax.broadcasted_iota(jnp.int32, (width, width), 0)
    second = lax.broadcasted_iota(jnp.int32, (width, width), 1)
    cell, slot = (second, first) if inverse else (first, second)
    half = width // 2
    source = jnp.where(slot < half, 2 * slot, 2 * (slot - half) + 1)
    return (cell == source).astype(F32).astype(BF16)


def later(row):
    lane = lax.broadcasted_iota(jnp.int32, row.shape, 1)
    return jnp.where(lane == 0, 0.0, pltpu.roll(row, 1, 1))


def earlier(row):
    lane = lax.broadcasted_iota(jnp.int32, row.shape, 1)
    last = row.shape[1] - 1
    return jnp.where(lane == last, 0.0, pltpu.roll(row, last, 1))


def gelu(value):
    return (0.5 * value) * (1.0 + jnp.tanh(value * (ROOT + ROOT * CUBIC * (value * value))))


def gelu_slope(value):
    square = value * value
    tanh = jnp.tanh(value * (ROOT + ROOT * CUBIC * square))
    inner = 0.5 * ROOT + 1.5 * ROOT * CUBIC * square
    return 0.5 + 0.5 * tanh + value * inner * (1.0 - tanh * tanh)


def forward_kernel(near_ref, own_ref, far_ref, wmid_ref, wtop_ref, cot_ref, delta_ref, pre_ref, vol_ref, pool_ref, *, h, w, spatial):
    half = w // 2
    here = lax.axis_index("spatial")
    first = here % 2 == 0
    split = parity_matrix(w, False)
    vrows = h + 2
    zero_row = jnp.zeros((vol_ref.shape[0], w), BF16)
    planes = []
    for part, ref in enumerate((near_ref, own_ref, near_ref)):
        for start in range(0, ref.shape[1], h * w):
            planes.append((part, start))
    channels = vol_ref.shape[0]
    for z, (part, start) in enumerate(planes):
        rows = []
        for at in range(start, start + h * w, w):
            if part == 1:
                rows.append(own_ref[:, at : at + w])
            else:
                rows.append(jnp.where(first == (part == 0), far_ref[:, at : at + w], near_ref[:, at : at + w]))
        rows = jnp.concatenate(rows, axis=0)
        sorted_rows = dot(rows, split).astype(BF16)
        base = z * vrows * w
        vol_ref[:, base : base + w] = zero_row
        vol_ref[:, base + (h + 1) * w : base + (h + 2) * w] = zero_row
        for y in range(h):
            vol_ref[:, base + (y + 1) * w : base + (y + 2) * w] = sorted_rows[y * channels : (y + 1) * channels]
    mid = pre_ref.shape[0]
    count = len(planes) - 2
    hp = h // 2
    prow = (hp + 2) * half
    pool_zero = jnp.zeros((pool_ref.shape[0], half), BF16)
    for pz in range(count // 2):
        sums = [None] * hp
        for j in (2 * pz, 2 * pz + 1):
            cols = jnp.concatenate(
                [vol_ref[:, ((j + a) * vrows + b) * w : ((j + a) * vrows + b + h) * w] for a in THREE for b in THREE],
                axis=0,
            )
            part = dot(wmid_ref[...], cols)
            for y in range(h):
                even = slice(y * w, y * w + half)
                odd = slice(y * w + half, (y + 1) * w)
                pre_even = part[mid : 2 * mid, even] + later(part[:mid, odd]) + part[2 * mid :, odd]
                pre_odd = part[mid : 2 * mid, odd] + part[:mid, even] + earlier(part[2 * mid :, even])
                if 0 < j < count - 1:
                    out = ((j - 1) * h + y) * w
                    pre_ref[:, out : out + half] = pre_even
                    pre_ref[:, out + half : out + w] = pre_odd
                both = gelu(pre_even) + gelu(pre_odd)
                sums[y // 2] = both if sums[y // 2] is None else sums[y // 2] + both
        base = pz * prow
        pool_ref[:, base : base + half] = pool_zero
        pool_ref[:, base + (hp + 1) * half : base + prow] = pool_zero
        for y in range(hp):
            row = sums[y] * 0.125
            if pz == 0:
                row = jnp.where(here == 0, 0.0, row)
            if pz == count // 2 - 1:
                row = jnp.where(here == spatial - 1, 0.0, row)
            row = row.astype(BF16).astype(F32)
            at = slice(base + (y + 1) * half, base + (y + 2) * half)
            pool_ref[:mid, at] = later(row).astype(BF16)
            pool_ref[mid : 2 * mid, at] = row.astype(BF16)
            pool_ref[2 * mid :, at] = earlier(row).astype(BF16)
    for j in range(count // 2 - 2):
        cols = jnp.concatenate(
            [pool_ref[:, (j + a) * prow + b * half : (j + a) * prow + (b + hp) * half] for a in THREE for b in THREE], axis=0
        )
        pre_top = dot(wtop_ref[...], cols, ((0,), (0,)))
        at = slice(j * hp * half, (j + 1) * hp * half)
        delta_ref[:, at] = (cot_ref[:, at].astype(F32) * gelu_slope(pre_top)).astype(BF16)


def halve(whole_ref, keep_ref, send_ref):
    core = lax.axis_index("spatial") % 2
    rows = keep_ref.shape[0]
    keep_ref[...] = whole_ref[pl.ds(pl.multiple_of(core * rows, 16), rows), :]
    sent = whole_ref[pl.ds(pl.multiple_of((1 - core) * rows, 16), rows), :].astype(BF16)
    send_ref[send_ref.shape[0] - rows :, :] = sent


def slope_kernel(pre_ref, slope_ref):
    for at in range(0, pre_ref.shape[1], 128):
        slope_ref[:, at : at + 128] = 0.125 * gelu_slope(pre_ref[:, at : at + 128])


def top_kernel(delta_ref, pool_ref, keep_ref, send_ref, out_ref, *, hp, wp):
    cout = delta_ref.shape[0]
    for at in range(0, delta_ref.shape[1], wp):
        send_ref[at // wp * cout : (at // wp + 1) * cout, :] = delta_ref[:, at : at + wp]
    prow = (hp + 2) * wp
    planes = delta_ref.shape[1] // (hp * wp)
    for a in THREE:
        for b in THREE:
            block = jnp.concatenate(
                [pool_ref[:, (j + a) * prow + b * wp : (j + a) * prow + (b + hp) * wp] for j in range(planes)], axis=1
            )
            rows = slice((3 * a + b) * block.shape[0], (3 * a + b + 1) * block.shape[0])
            out_ref[rows, :] = dot(block, delta_ref[...], ((1,), (1,)))
    halve(out_ref, keep_ref, send_ref)


def backward_kernel(
    near_ref, own_ref, far_ref, slope_ref, vol_ref, wtop_ref, keep_ref, send_ref, field_ref, top_ref, shift_ref, mid_ref, *, h, w, spatial
):
    half, hp = w // 2, h // 2
    here = lax.axis_index("spatial")
    trow = (hp + 2) * half
    top_zero = jnp.zeros((top_ref.shape[0], half), BF16)
    depth = own_ref.shape[1] // (hp * half)
    for z in range(3 * depth):
        start = (z % depth) * hp * half
        at = slice(start, start + hp * half)
        if z // depth == 1:
            plane = own_ref[:, at]
        else:
            cout = own_ref.shape[0]
            blocks = range((z % depth) * hp, (z % depth + 1) * hp)
            near = jnp.concatenate([near_ref[k * cout : (k + 1) * cout, :] for k in blocks], axis=1)
            plane = jnp.where((here % 2 == 0) == (z < depth), far_ref[:, at], near)
        base = z * trow
        top_ref[:, base : base + half] = top_zero
        top_ref[:, base + half : base + (hp + 1) * half] = plane
        top_ref[:, base + (hp + 1) * half : base + trow] = top_zero
    mid = slope_ref.shape[0]
    weights = jnp.concatenate(
        [
            jnp.concatenate([wtop_ref[(3 * ab + c) * mid : (3 * ab + c + 1) * mid, :] for ab in range(9)], axis=1)
            for c in THREE
        ],
        axis=0,
    )
    outer = depth + 2
    first = depth - 1
    cols = jnp.concatenate(
        [
            jnp.concatenate(
                [
                    top_ref[:, (first + j + 1 - a) * trow + (2 - b) * half : (first + j + 1 - a) * trow + (2 - b + hp) * half]
                    for j in range(outer)
                ],
                axis=1,
            )
            for a in THREE
            for b in THREE
        ],
        axis=0,
    )
    part = dot(weights, cols)
    vrows = h + 2
    field_zero = jnp.zeros((mid, w), BF16)
    fine = 2 * depth
    for m in range(fine + 2):
        j = (m + 1) // 2
        base = m * vrows * w
        field_ref[:, base : base + w] = field_zero
        field_ref[:, base + (h + 1) * w : base + vrows * w] = field_zero
        for y in range(h):
            at = slice((j * hp + y // 2) * half, (j * hp + y // 2 + 1) * half)
            pool = part[mid : 2 * mid, at] + later(part[2 * mid :, at]) + earlier(part[:mid, at])
            if m == 0:
                pool = jnp.where(here == 0, 0.0, pool)
            if m == fine + 1:
                pool = jnp.where(here == spatial - 1, 0.0, pool)
            out = (m * h + y) * w
            even = (slope_ref[:, out : out + half] * pool).astype(BF16)
            odd = (slope_ref[:, out + half : out + w] * pool).astype(BF16)
            to = base + (y + 1) * w
            field_ref[:, to : to + half] = even
            field_ref[:, to + half : to + w] = odd
            if 0 < m <= fine:
                to = ((m - 1) * h + y) * w
                shift_ref[:mid, to : to + half] = odd
                shift_ref[:mid, to + half : to + w] = earlier(even.astype(F32)).astype(BF16)
                shift_ref[mid : 2 * mid, to : to + half] = even
                shift_ref[mid : 2 * mid, to + half : to + w] = odd
                shift_ref[2 * mid :, to : to + half] = later(odd.astype(F32)).astype(BF16)
                shift_ref[2 * mid :, to + half : to + w] = even
    total = None
    for z in range(fine):
        piece = jnp.concatenate(
            [
                vol_ref[:, ((z + 2 + a) * vrows + b) * w : ((z + 2 + a) * vrows + b + h) * w]
                for a in THREE
                for b in THREE
            ],
            axis=0,
        )
        product = dot(piece, shift_ref[:, z * h * w : (z + 1) * h * w], ((1,), (1,)))
        total = product if total is None else total + product
    rows = total.shape[0]
    half_rows = rows // 2
    mid_ref[:rows, :] = total[:, : 2 * mid]
    last = total[:, 2 * mid :]
    mid_ref[rows : rows + half_rows, :] = jnp.concatenate([last[:half_rows], last[half_rows:]], axis=1)
    spare = mid_ref.shape[0] - rows - half_rows
    if spare:
        mid_ref[rows + half_rows :, :] = jnp.zeros((spare, 2 * mid), F32)
    halve(mid_ref, keep_ref, send_ref)


def input_kernel(field_ref, wback_ref, out_ref, *, h, w):
    half = w // 2
    vrows = h + 2
    join = parity_matrix(w, True)
    ch = out_ref.shape[0]
    for z in range(out_ref.shape[1] // (h * w)):
        cols = jnp.concatenate(
            [
                field_ref[:, ((z + 2 - a) * vrows + 2 - b) * w : ((z + 2 - a) * vrows + 2 - b + h) * w]
                for a in THREE
                for b in THREE
            ],
            axis=0,
        )
        part = dot(wback_ref[...], cols)
        rows = []
        for y in range(h):
            even = slice(y * w, y * w + half)
            odd = slice(y * w + half, (y + 1) * w)
            grad_even = part[ch : 2 * ch, even] + later(part[2 * ch :, odd]) + part[:ch, odd]
            grad_odd = part[ch : 2 * ch, odd] + part[2 * ch :, even] + earlier(part[:ch, even])
            rows.append(jnp.concatenate([grad_even, grad_odd], axis=1).astype(BF16))
        joined = dot(jnp.concatenate(rows, axis=0), join).astype(BF16)
        for y in range(h):
            out_ref[:, (z * h + y) * w : (z * h + y + 1) * w] = joined[y * ch : (y + 1) * ch]


def finish_kernel(own_ref, other_ref, top_ref, mid_ref, *, scale_top, scale_mid):
    core = lax.axis_index("spatial") % 2
    top_rows = top_ref.shape[0] // 2
    top_ref[pl.ds(pl.multiple_of(core * top_rows, 16), top_rows), :] = own_ref[:top_rows].astype(F32) * scale_top
    top_ref[pl.ds(pl.multiple_of((1 - core) * top_rows, 16), top_rows), :] = other_ref[:top_rows].astype(F32) * scale_top
    mid_rows = (own_ref.shape[0] - top_rows) // 2
    own = own_ref[top_rows : top_rows + mid_rows].astype(F32) + own_ref[top_rows + mid_rows :].astype(F32)
    other = other_ref[top_rows : top_rows + mid_rows].astype(F32) + other_ref[top_rows + mid_rows :].astype(F32)
    low = jnp.where(core == 0, own, other)
    high = jnp.where(core == 0, other, own)
    whole = jnp.concatenate([low, high], axis=0) * scale_mid
    rows = mid_ref.shape[0] // 3
    mid = mid_ref.shape[1]
    q = rows // 9
    for ab in range(9):
        block = whole[ab * q : (ab + 1) * q]
        mid_ref[(3 * ab) * q : (3 * ab + 1) * q, :] = block[:, :mid]
        mid_ref[(3 * ab + 1) * q : (3 * ab + 2) * q, :] = block[:, mid:]
    half_rows = rows // 2
    last = whole[rows : rows + half_rows]
    last = jnp.concatenate([last[:, :mid], last[:, mid:]], axis=0)
    for ab in range(9):
        mid_ref[(3 * ab + 2) * q : (3 * ab + 3) * q, :] = last[ab * q : (ab + 1) * q]


def partner(block, bit):
    size = lax.axis_size("spatial")
    return lax.ppermute(block, "spatial", [(i, i ^ bit) for i in range(size)])


def across(block):
    size = lax.axis_size("spatial")
    pairs = [(i, i + 1) for i in range(1, size - 1, 2)]
    return lax.ppermute(block, "spatial", pairs + [(j, i) for i, j in pairs])


def bit_is_clear(bit):
    return (lax.axis_index("spatial") & bit) == 0


def rounded(block):
    return lax.optimization_barrier(block.astype(BF16))


def add_both(sent, bit):
    return sent.astype(F32) + partner(sent, bit).astype(F32)


def halves(block, low):
    rows = block.shape[0] // 2
    mine = jnp.where(low, block[:rows], block[rows:])
    other = jnp.where(low, block[rows:], block[:rows])
    return mine, rounded(other)


def in_order(block, other, low):
    return jnp.where(low, block, other), jnp.where(low, other, block)


def far_bits():
    return [1 << k for k in range(2, lax.axis_size("spatial").bit_length() - 1)]


def shards(volume, weights_mid, weights_top, cotangent):
    spatial = lax.axis_size("spatial")
    cin, nz, h, w = volume.shape
    mid = weights_mid.shape[0]
    cout, nzp, hp, wp = cotangent.shape
    shape = jax.ShapeDtypeStruct
    plane = h * w
    volume, first_core, low = lax.optimization_barrier((volume, bit_is_clear(1), bit_is_clear(2)))
    flat = volume.reshape(cin, nz * plane)
    early, late = flat[:, : (nz - 1) * plane], flat[:, plane:]
    far = across(jnp.where(first_core, early, late))
    near = partner(jnp.where(first_core, late, early), 1)
    split = weights_mid.reshape(mid, 9, 3, cin)
    wmid = jnp.transpose(split, (2, 0, 1, 3)).reshape(3 * mid, 9 * cin)
    wback = jnp.transpose(split, (2, 3, 1, 0)).reshape(3 * cin, 9 * mid)
    wtop = jnp.transpose(weights_top, (1, 2, 0)).reshape(27 * mid, cout)
    cot = cotangent.reshape(cout, nzp * hp * wp)
    near, far, wback = lax.optimization_barrier((near, far, wback))
    padded = (3 * nz - 2) * (h + 2) * w
    delta, pre, vol, pool = kernel_call(
        lambda *refs: forward_kernel(*refs, h=h, w=w, spatial=spatial),
        "forward",
        (
            shape(cot.shape, BF16),
            shape((mid, (nz + 2) * plane), F32),
            shape((cin, padded), BF16),
            shape((3 * mid, (nzp + 2) * (hp + 2) * wp), BF16),
        ),
        (near, flat, far, wmid, wtop, cot),
        flops=1_200_000_000,
        moved=6_000_000,
    )
    delta_far = across(delta)
    top_rows = 27 * mid
    delta_rows = delta.size // cout
    keep, send = kernel_call(
        lambda *refs: top_kernel(*refs, hp=hp, wp=wp),
        "top_part",
        (shape((top_rows // 2, cout), F32), shape((delta_rows + top_rows // 2, cout), BF16)),
        (delta, pool),
        scratch=(pltpu.VMEM((top_rows, cout), F32),),
        flops=226_000_000,
        moved=1_500_000,
    )
    slope = kernel_call(slope_kernel, "slope", shape(pre.shape, F32), (pre,), flops=100_000_000, moved=3_000_000)
    delta_near = partner(send, 1)
    mine, other = halves(keep + delta_near[delta_rows:].astype(F32), low)
    top_received = partner(other, 2)
    mid_rows = -(-27 * cin // 64) * 16
    keep, send, field = kernel_call(
        lambda *refs: backward_kernel(*refs, h=h, w=w, spatial=spatial),
        "backward",
        (
            shape((mid_rows, 2 * mid), F32),
            shape((mid_rows, 2 * mid), BF16),
            shape((mid, (nz + 2) * (h + 2) * w), BF16),
        ),
        (delta_near, delta, delta_far, slope, vol, wtop),
        scratch=(
            pltpu.VMEM((cout, 3 * nzp * (hp + 2) * wp), BF16),
            pltpu.VMEM((3 * mid, nz * plane), BF16),
            pltpu.VMEM((2 * mid_rows, 2 * mid), F32),
        ),
        flops=900_000_000,
        moved=5_000_000,
    )
    keep, send, mine, top_received = lax.optimization_barrier((keep, send, mine, top_received))
    top_sum = rounded(mine + top_received.astype(F32))
    bits = far_bits()
    top_sum = rounded(add_both(top_sum, bits[0]))
    for bit in bits[1:]:
        top_sum = rounded(add_both(top_sum, bit))
    mid_sum = rounded(keep + partner(send, 1).astype(F32))
    for bit in bits:
        mid_sum = rounded(add_both(mid_sum, bit))
        if bit == bits[0]:
            mid_sum, field = lax.optimization_barrier((mid_sum, field))
    input_grad = kernel_call(
        lambda *refs: input_kernel(*refs, h=h, w=w),
        "input_grad",
        shape((cin, nz * plane), BF16),
        (field, wback),
        flops=452_000_000,
        moved=2_000_000,
    )
    both = jnp.concatenate([top_sum, mid_sum], axis=0)
    both, input_grad = lax.optimization_barrier((both, input_grad))
    received = partner(both, 2)
    top_sum = jnp.concatenate(in_order(top_sum, received[: top_sum.shape[0]], low), axis=0)
    mid_sum = mid_sum.astype(F32) + received[-mid_rows:].astype(F32)
    mid_high = rounded(mid_sum)
    mid_low = rounded(mid_sum - mid_high.astype(F32))
    both = jnp.concatenate([top_sum, mid_high, mid_low], axis=0)
    top_grad, mid_grad = kernel_call(
        lambda *refs: finish_kernel(
            *refs,
            scale_top=1.0 / math.sqrt(nzp * hp * wp * spatial),
            scale_mid=1.0 / math.sqrt(nz * plane * spatial),
        ),
        "finish",
        (shape((27 * mid, cout), F32), shape((27 * cin, mid), F32)),
        (both, partner(both, 1)),
        moved=2_000_000,
        last=True,
    )
    return (
        input_grad.reshape(volume.shape),
        jnp.transpose(mid_grad.reshape(27, cin, mid), (2, 0, 1)),
        jnp.transpose(top_grad.reshape(27, mid, cout), (2, 0, 1)),
    )


def solution(mesh):
    return jax.shard_map(
        shards,
        mesh=mesh,
        in_specs=(P(None, "spatial", "groups", None), P(), P(), P(None, "spatial", "groups", None)),
        out_specs=(
            P(None, "spatial", "groups", None),
            P("groups", None, None),
            P("groups", None, None),
        ),
        check_vma=False,
    )
```

```python
import math

import jax
import jax.numpy as jnp
from jax import lax
from jax.experimental import pallas as pl
from jax.experimental.pallas import tpu as pltpu
from jax.sharding import PartitionSpec as P

BF16 = jnp.bfloat16
F32 = jnp.float32
ROOT = math.sqrt(2.0 / math.pi)
CUBIC = 0.044715
THREE = (0, 1, 2)
VMEM_LIMIT = 20 << 20


def kernel_call(body, name, outs, args, scratch=(), flops=0, moved=0, last=False):
    whole = pl.BlockSpec(memory_space=pltpu.VMEM)
    args = [pltpu.with_memory_space_constraint(arg, pltpu.VMEM) for arg in args]
    if not last:
        outs = jax.tree.map(lambda out: pltpu.VMEM(out.shape, out.dtype), outs)
    return pl.pallas_call(
        body,
        name=name,
        out_shape=outs,
        in_specs=[whole] * len(args),
        out_specs=jax.tree.map(lambda _: whole, outs),
        scratch_shapes=list(scratch),
        compiler_params=pltpu.CompilerParams(vmem_limit_bytes=VMEM_LIMIT),
        cost_estimate=pl.CostEstimate(flops=flops, bytes_accessed=moved, transcendentals=0),
    )(*args)


def dot(a, b, contract=((1,), (0,))):
    return lax.dot_general(a, b, (contract, ((), ())), preferred_element_type=F32)


def parity_matrix(width, inverse):
    first = lax.broadcasted_iota(jnp.int32, (width, width), 0)
    second = lax.broadcasted_iota(jnp.int32, (width, width), 1)
    cell, slot = (second, first) if inverse else (first, second)
    half = width // 2
    source = jnp.where(slot < half, 2 * slot, 2 * (slot - half) + 1)
    return (cell == source).astype(F32).astype(BF16)


def later(row):
    lane = lax.broadcasted_iota(jnp.int32, row.shape, 1)
    return jnp.where(lane == 0, 0.0, pltpu.roll(row, 1, 1))


def earlier(row):
    lane = lax.broadcasted_iota(jnp.int32, row.shape, 1)
    last = row.shape[1] - 1
    return jnp.where(lane == last, 0.0, pltpu.roll(row, last, 1))


def gelu(value):
    return (0.5 * value) * (1.0 + jnp.tanh(value * (ROOT + ROOT * CUBIC * (value * value))))


def gelu_slope(value):
    square = value * value
    tanh = jnp.tanh(value * (ROOT + ROOT * CUBIC * square))
    inner = 0.5 * ROOT + 1.5 * ROOT * CUBIC * square
    return 0.5 + 0.5 * tanh + value * inner * (1.0 - tanh * tanh)


def sort_plane(rows, split, store, h, w):
    channels = rows[0].shape[0]
    done = dot(jnp.concatenate(rows, axis=0), split).astype(BF16)
    store(0, jnp.zeros((channels, w), BF16))
    store(h + 1, jnp.zeros((channels, w), BF16))
    for y in range(h):
        store(y + 1, done[y * channels : (y + 1) * channels])


def lanes(start, size):
    return pl.ds(pl.multiple_of(start, 128), size)


def middle_planes(vol_ref, wmid_ref, pre_ref, begin, count, h, w, emit):
    half = w // 2
    mid = pre_ref.shape[0]
    for pz in range(count // 2):
        sums = [None] * (h // 2)
        for j in (2 * pz, 2 * pz + 1):
            at = (begin + j) * (h + 2) * w
            cols = jnp.concatenate([vol_ref[:, lanes(at + (a * (h + 2) + b) * w, h * w)] for a in THREE for b in THREE], axis=0)
            part = dot(wmid_ref[...], cols)
            for y in range(h):
                even = slice(y * w, y * w + half)
                odd = slice(y * w + half, (y + 1) * w)
                pre_even = part[mid : 2 * mid, even] + later(part[:mid, odd]) + part[2 * mid :, odd]
                pre_odd = part[mid : 2 * mid, odd] + part[:mid, even] + earlier(part[2 * mid :, even])
                out = (j * h + y) * w
                pre_ref[:, out : out + half] = pre_even
                pre_ref[:, out + half : out + w] = pre_odd
                both = gelu(pre_even) + gelu(pre_odd)
                sums[y // 2] = both if sums[y // 2] is None else sums[y // 2] + both
        emit(pz, [row * 0.125 for row in sums])


def pool_rows(pool_ref, base, rows, outside):
    mid, half = rows[0].shape
    zero = jnp.zeros((3 * mid, half), BF16)
    pool_ref[:, lanes(base, half)] = zero
    pool_ref[:, lanes(base + (len(rows) + 1) * half, half)] = zero
    for y, row in enumerate(rows):
        row = jnp.where(outside, 0.0, row).astype(BF16)
        wide = row.astype(F32)
        at = lanes(base + (y + 1) * half, half)
        pool_ref[:mid, at] = later(wide).astype(BF16)
        pool_ref[mid : 2 * mid, at] = row
        pool_ref[2 * mid :, at] = earlier(wide).astype(BF16)


def near_kernel(near_ref, own_ref, wmid_ref, vol_ref, pre_ref, pool_ref, *, h, w, spatial):
    here = lax.axis_index("spatial")
    core = here % 2
    split = parity_matrix(w, False)
    size = (h + 2) * w
    halo = near_ref.shape[1] // (h * w)
    own = own_ref.shape[1] // (h * w)
    for ref, count, start in ((own_ref, own, core * halo), (near_ref, halo, (1 - core) * own)):
        for z in range(count):
            rows = [ref[:, (z * h + y) * w : (z * h + y + 1) * w] for y in range(h)]

            def store(row, value, at=(start + z) * size):
                vol_ref[:, lanes(at + row * w, w)] = value

            sort_plane(rows, split, store, h, w)
    count = pre_ref.shape[1] // (h * w)
    pooled = count // 2
    prow = pool_ref.shape[1] // pooled

    def emit(pz, rows):
        first = (core == 1) & (here == 0) if pz == 0 else False
        last = (core == 0) & (here == spatial - 1) if pz == pooled - 1 else False
        pool_rows(pool_ref, pz * prow, rows, jnp.logical_or(first, last))

    middle_planes(vol_ref, wmid_ref, pre_ref, 1 - core, count, h, w, emit)


def far_kernel(
    far_ref, vol_near_ref, pool_near_ref, wmid_ref, wtop_ref, cot_ref, delta_ref, pre_ref, vol_ref, pool_ref, *, h, w, spatial
):
    half = w // 2
    here = lax.axis_index("spatial")
    core = here % 2
    split = parity_matrix(w, False)
    size = (h + 2) * w
    halo = far_ref.shape[1] // (h * w)
    known = vol_near_ref.shape[1]
    vol_ref[:, lanes((1 - core) * halo * size, known)] = vol_near_ref[...]
    for z in range(halo):
        rows = [far_ref[:, (z * h + y) * w : (z * h + y + 1) * w] for y in range(h)]

        def store(row, value, at=core * known + z * size):
            vol_ref[:, lanes(at + row * w, w)] = value

        sort_plane(rows, split, store, h, w)
    count = pre_ref.shape[1] // (h * w)
    pooled = count // 2
    hp = h // 2
    prow = (hp + 2) * half
    pool_ref[:, lanes((1 - core) * pooled * prow, pooled * prow)] = pool_near_ref[...]

    def emit(pz, rows):
        first = (core == 0) & (here == 0) if pz == 0 else False
        last = (core == 1) & (here == spatial - 1) if pz == pooled - 1 else False
        pool_rows(pool_ref, (core * pooled + pz) * prow, rows, jnp.logical_or(first, last))

    middle_planes(vol_ref, wmid_ref, pre_ref, core * count, count, h, w, emit)
    for j in range(delta_ref.shape[1] // (hp * half)):
        cols = jnp.concatenate(
            [pool_ref[:, (j + a) * prow + b * half : (j + a) * prow + (b + hp) * half] for a in THREE for b in THREE], axis=0
        )
        pre_top = dot(wtop_ref[...], cols, ((0,), (0,)))
        at = slice(j * hp * half, (j + 1) * hp * half)
        delta_ref[:, at] = (cot_ref[:, at].astype(F32) * gelu_slope(pre_top)).astype(BF16)


def halve(whole_ref, keep_ref, send_ref):
    core = lax.axis_index("spatial") % 2
    rows = keep_ref.shape[0]
    keep_ref[...] = whole_ref[pl.ds(pl.multiple_of(core * rows, 16), rows), :]
    sent = whole_ref[pl.ds(pl.multiple_of((1 - core) * rows, 16), rows), :].astype(BF16)
    send_ref[send_ref.shape[0] - rows :, :] = sent


def slope_kernel(near_ref, far_ref, slope_ref, *, plane):
    core = lax.axis_index("spatial") % 2
    part = slope_ref.shape[1] // 2
    for ref, side in ((near_ref, 1 - core), (far_ref, core)):
        for at in range(0, part, 128):
            value = 0.125 * gelu_slope(ref[:, lanes((1 - side) * plane + at, 128)])
            slope_ref[:, lanes(side * part + at, 128)] = value


def top_kernel(delta_ref, pool_ref, keep_ref, send_ref, out_ref, *, hp, wp):
    cout = delta_ref.shape[0]
    for at in range(0, delta_ref.shape[1], wp):
        send_ref[at // wp * cout : (at // wp + 1) * cout, :] = delta_ref[:, at : at + wp]
    prow = (hp + 2) * wp
    planes = delta_ref.shape[1] // (hp * wp)
    for a in THREE:
        for b in THREE:
            block = jnp.concatenate(
                [pool_ref[:, (j + a) * prow + b * wp : (j + a) * prow + (b + hp) * wp] for j in range(planes)], axis=1
            )
            rows = slice((3 * a + b) * block.shape[0], (3 * a + b + 1) * block.shape[0])
            out_ref[rows, :] = dot(block, delta_ref[...], ((1,), (1,)))
    halve(out_ref, keep_ref, send_ref)


def backward_kernel(
    near_ref, own_ref, far_ref, slope_ref, vol_ref, wtop_ref, keep_ref, send_ref, field_ref, top_ref, shift_ref, mid_ref, *, h, w, spatial
):
    half, hp = w // 2, h // 2
    here = lax.axis_index("spatial")
    trow = (hp + 2) * half
    top_zero = jnp.zeros((top_ref.shape[0], half), BF16)
    depth = own_ref.shape[1] // (hp * half)
    for z in range(3 * depth):
        start = (z % depth) * hp * half
        at = slice(start, start + hp * half)
        if z // depth == 1:
            plane = own_ref[:, at]
        else:
            cout = own_ref.shape[0]
            blocks = range((z % depth) * hp, (z % depth + 1) * hp)
            near = jnp.concatenate([near_ref[k * cout : (k + 1) * cout, :] for k in blocks], axis=1)
            plane = jnp.where((here % 2 == 0) == (z < depth), far_ref[:, at], near)
        base = z * trow
        top_ref[:, base : base + half] = top_zero
        top_ref[:, base + half : base + (hp + 1) * half] = plane
        top_ref[:, base + (hp + 1) * half : base + trow] = top_zero
    mid = slope_ref.shape[0]
    weights = jnp.concatenate(
        [
            jnp.concatenate([wtop_ref[(3 * ab + c) * mid : (3 * ab + c + 1) * mid, :] for ab in range(9)], axis=1)
            for c in THREE
        ],
        axis=0,
    )
    outer = depth + 2
    first = depth - 1
    cols = jnp.concatenate(
        [
            jnp.concatenate(
                [
                    top_ref[:, (first + j + 1 - a) * trow + (2 - b) * half : (first + j + 1 - a) * trow + (2 - b + hp) * half]
                    for j in range(outer)
                ],
                axis=1,
            )
            for a in THREE
            for b in THREE
        ],
        axis=0,
    )
    part = dot(weights, cols)
    vrows = h + 2
    field_zero = jnp.zeros((mid, w), BF16)
    fine = 2 * depth
    for m in range(fine + 2):
        j = (m + 1) // 2
        base = m * vrows * w
        field_ref[:, base : base + w] = field_zero
        field_ref[:, base + (h + 1) * w : base + vrows * w] = field_zero
        for y in range(h):
            at = slice((j * hp + y // 2) * half, (j * hp + y // 2 + 1) * half)
            pool = part[mid : 2 * mid, at] + later(part[2 * mid :, at]) + earlier(part[:mid, at])
            if m == 0:
                pool = jnp.where(here == 0, 0.0, pool)
            if m == fine + 1:
                pool = jnp.where(here == spatial - 1, 0.0, pool)
            out = (m * h + y) * w
            even = (slope_ref[:, out : out + half] * pool).astype(BF16)
            odd = (slope_ref[:, out + half : out + w] * pool).astype(BF16)
            to = base + (y + 1) * w
            field_ref[:, to : to + half] = even
            field_ref[:, to + half : to + w] = odd
            if 0 < m <= fine:
                to = ((m - 1) * h + y) * w
                shift_ref[:mid, to : to + half] = odd
                shift_ref[:mid, to + half : to + w] = earlier(even.astype(F32)).astype(BF16)
                shift_ref[mid : 2 * mid, to : to + half] = even
                shift_ref[mid : 2 * mid, to + half : to + w] = odd
                shift_ref[2 * mid :, to : to + half] = later(odd.astype(F32)).astype(BF16)
                shift_ref[2 * mid :, to + half : to + w] = even
    total = None
    for z in range(fine):
        piece = jnp.concatenate(
            [
                vol_ref[:, ((z + 2 + a) * vrows + b) * w : ((z + 2 + a) * vrows + b + h) * w]
                for a in THREE
                for b in THREE
            ],
            axis=0,
        )
        product = dot(piece, shift_ref[:, z * h * w : (z + 1) * h * w], ((1,), (1,)))
        total = product if total is None else total + product
    rows = total.shape[0]
    half_rows = rows // 2
    mid_ref[:rows, :] = total[:, : 2 * mid]
    last = total[:, 2 * mid :]
    mid_ref[rows : rows + half_rows, :] = jnp.concatenate([last[:half_rows], last[half_rows:]], axis=1)
    spare = mid_ref.shape[0] - rows - half_rows
    if spare:
        mid_ref[rows + half_rows :, :] = jnp.zeros((spare, 2 * mid), F32)
    halve(mid_ref, keep_ref, send_ref)


def input_kernel(field_ref, wback_ref, out_ref, *, h, w):
    half = w // 2
    vrows = h + 2
    join = parity_matrix(w, True)
    ch = out_ref.shape[0]
    for z in range(out_ref.shape[1] // (h * w)):
        cols = jnp.concatenate(
            [
                field_ref[:, ((z + 2 - a) * vrows + 2 - b) * w : ((z + 2 - a) * vrows + 2 - b + h) * w]
                for a in THREE
                for b in THREE
            ],
            axis=0,
        )
        part = dot(wback_ref[...], cols)
        rows = []
        for y in range(h):
            even = slice(y * w, y * w + half)
            odd = slice(y * w + half, (y + 1) * w)
            grad_even = part[ch : 2 * ch, even] + later(part[2 * ch :, odd]) + part[:ch, odd]
            grad_odd = part[ch : 2 * ch, odd] + part[2 * ch :, even] + earlier(part[:ch, even])
            rows.append(jnp.concatenate([grad_even, grad_odd], axis=1).astype(BF16))
        joined = dot(jnp.concatenate(rows, axis=0), join).astype(BF16)
        for y in range(h):
            out_ref[:, (z * h + y) * w : (z * h + y + 1) * w] = joined[y * ch : (y + 1) * ch]


def finish_kernel(own_ref, other_ref, top_ref, mid_ref, *, scale_top, scale_mid):
    core = lax.axis_index("spatial") % 2
    top_rows = top_ref.shape[0] // 2
    top_ref[pl.ds(pl.multiple_of(core * top_rows, 16), top_rows), :] = own_ref[:top_rows].astype(F32) * scale_top
    top_ref[pl.ds(pl.multiple_of((1 - core) * top_rows, 16), top_rows), :] = other_ref[:top_rows].astype(F32) * scale_top
    mid_rows = (own_ref.shape[0] - top_rows) // 2
    own = own_ref[top_rows : top_rows + mid_rows].astype(F32) + own_ref[top_rows + mid_rows :].astype(F32)
    other = other_ref[top_rows : top_rows + mid_rows].astype(F32) + other_ref[top_rows + mid_rows :].astype(F32)
    low = jnp.where(core == 0, own, other)
    high = jnp.where(core == 0, other, own)
    whole = jnp.concatenate([low, high], axis=0) * scale_mid
    rows = mid_ref.shape[0] // 3
    mid = mid_ref.shape[1]
    q = rows // 9
    for ab in range(9):
        block = whole[ab * q : (ab + 1) * q]
        mid_ref[(3 * ab) * q : (3 * ab + 1) * q, :] = block[:, :mid]
        mid_ref[(3 * ab + 1) * q : (3 * ab + 2) * q, :] = block[:, mid:]
    half_rows = rows // 2
    last = whole[rows : rows + half_rows]
    last = jnp.concatenate([last[:, :mid], last[:, mid:]], axis=0)
    for ab in range(9):
        mid_ref[(3 * ab + 2) * q : (3 * ab + 3) * q, :] = last[ab * q : (ab + 1) * q]


def partner(block, bit):
    size = lax.axis_size("spatial")
    return lax.ppermute(block, "spatial", [(i, i ^ bit) for i in range(size)])


def across(block):
    size = lax.axis_size("spatial")
    pairs = [(i, i + 1) for i in range(1, size - 1, 2)]
    return lax.ppermute(block, "spatial", pairs + [(j, i) for i, j in pairs])


def bit_is_clear(bit):
    return (lax.axis_index("spatial") & bit) == 0


def rounded(block):
    return lax.optimization_barrier(block.astype(BF16))


def add_both(sent, bit):
    return sent.astype(F32) + partner(sent, bit).astype(F32)


def halves(block, low):
    rows = block.shape[0] // 2
    mine = jnp.where(low, block[:rows], block[rows:])
    other = jnp.where(low, block[rows:], block[:rows])
    return mine, rounded(other)


def in_order(block, other, low):
    return jnp.where(low, block, other), jnp.where(low, other, block)


def far_bits():
    return [1 << k for k in range(2, lax.axis_size("spatial").bit_length() - 1)]


def shards(volume, weights_mid, weights_top, cotangent):
    spatial = lax.axis_size("spatial")
    cin, nz, h, w = volume.shape
    mid = weights_mid.shape[0]
    cout, nzp, hp, wp = cotangent.shape
    shape = jax.ShapeDtypeStruct
    plane = h * w
    volume, first_core, low = lax.optimization_barrier((volume, bit_is_clear(1), bit_is_clear(4)))
    flat = volume.reshape(cin, nz * plane)
    early, late = flat[:, : (nz - 1) * plane], flat[:, plane:]
    far = across(jnp.where(first_core, early, late))
    near = partner(jnp.where(first_core, late, early), 1)
    split = weights_mid.reshape(mid, 9, 3, cin)
    wmid = jnp.transpose(split, (2, 0, 1, 3)).reshape(3 * mid, 9 * cin)
    wback = jnp.transpose(split, (2, 3, 1, 0)).reshape(3 * cin, 9 * mid)
    wtop = jnp.transpose(weights_top, (1, 2, 0)).reshape(27 * mid, cout)
    cot = cotangent.reshape(cout, nzp * hp * wp)
    size = (h + 2) * w
    count = nz // 2 + 2
    halo = nz - 1
    pool_size = (hp + 2) * wp
    vol_near, pre_near, pool_near = kernel_call(
        lambda *refs: near_kernel(*refs, h=h, w=w, spatial=spatial),
        "near_side",
        (
            shape((cin, (nz + halo) * size), BF16),
            shape((mid, count * plane), F32),
            shape((3 * mid, count // 2 * pool_size), BF16),
        ),
        (near, flat, wmid),
        flops=900_000_000,
        moved=3_000_000,
    )
    far, wback, vol_near, pool_near = lax.optimization_barrier((far, wback, vol_near, pool_near))
    delta, pre_far, vol, pool = kernel_call(
        lambda *refs: far_kernel(*refs, h=h, w=w, spatial=spatial),
        "far_side",
        (
            shape(cot.shape, BF16),
            shape((mid, count * plane), F32),
            shape((cin, (nz + 2 * halo) * size), BF16),
            shape((3 * mid, count * pool_size), BF16),
        ),
        (far, vol_near, pool_near, wmid, wtop, cot),
        flops=900_000_000,
        moved=4_000_000,
    )
    delta_far = across(delta)
    top_rows = 27 * mid
    delta_rows = delta.size // cout
    keep, send = kernel_call(
        lambda *refs: top_kernel(*refs, hp=hp, wp=wp),
        "top_part",
        (shape((top_rows // 2, cout), F32), shape((delta_rows + top_rows // 2, cout), BF16)),
        (delta, pool),
        scratch=(pltpu.VMEM((top_rows, cout), F32),),
        flops=226_000_000,
        moved=1_500_000,
    )
    slope = kernel_call(
        lambda *refs: slope_kernel(*refs, plane=plane),
        "slope",
        shape((mid, (nz + 2) * plane), F32),
        (pre_near, pre_far),
        flops=100_000_000,
        moved=3_000_000,
    )
    delta_near = partner(send, 1)
    mine, other = halves(keep + delta_near[delta_rows:].astype(F32), low)
    top_received = partner(other, 4)
    mid_rows = -(-27 * cin // 64) * 16
    keep, send, field = kernel_call(
        lambda *refs: backward_kernel(*refs, h=h, w=w, spatial=spatial),
        "backward",
        (
            shape((mid_rows, 2 * mid), F32),
            shape((mid_rows, 2 * mid), BF16),
            shape((mid, (nz + 2) * (h + 2) * w), BF16),
        ),
        (delta_near, delta, delta_far, slope, vol, wtop),
        scratch=(
            pltpu.VMEM((cout, 3 * nzp * (hp + 2) * wp), BF16),
            pltpu.VMEM((3 * mid, nz * plane), BF16),
            pltpu.VMEM((2 * mid_rows, 2 * mid), F32),
        ),
        flops=900_000_000,
        moved=5_000_000,
    )
    keep, send, mine, top_received = lax.optimization_barrier((keep, send, mine, top_received))
    top_sum = rounded(mine + top_received.astype(F32))
    bits = far_bits()[1:]
    top_sum, send = lax.optimization_barrier((top_sum, send))
    for bit in bits:
        top_sum = rounded(add_both(top_sum, bit))
    mid_sum = rounded(keep + partner(send, 1).astype(F32))
    mid_sum = rounded(add_both(mid_sum, 2))
    top_sum, mid_sum = lax.optimization_barrier((top_sum, mid_sum))
    mid_sum, field = lax.optimization_barrier((mid_sum, field))
    for bit in bits:
        mid_sum = rounded(add_both(mid_sum, bit))
    top_sum = rounded(add_both(top_sum, 2))
    input_grad = kernel_call(
        lambda *refs: input_kernel(*refs, h=h, w=w),
        "input_grad",
        shape((cin, nz * plane), BF16),
        (field, wback),
        flops=452_000_000,
        moved=2_000_000,
    )
    both = jnp.concatenate([top_sum, mid_sum], axis=0)
    both, input_grad = lax.optimization_barrier((both, input_grad))
    received = partner(both, 4)
    top_sum = jnp.concatenate(in_order(top_sum, received[: top_sum.shape[0]], low), axis=0)
    mid_sum = mid_sum.astype(F32) + received[-mid_rows:].astype(F32)
    mid_high = rounded(mid_sum)
    mid_low = rounded(mid_sum - mid_high.astype(F32))
    both = jnp.concatenate([top_sum, mid_high, mid_low], axis=0)
    top_grad, mid_grad = kernel_call(
        lambda *refs: finish_kernel(
            *refs,
            scale_top=1.0 / math.sqrt(nzp * hp * wp * spatial),
            scale_mid=1.0 / math.sqrt(nz * plane * spatial),
        ),
        "finish",
        (shape((27 * mid, cout), F32), shape((27 * cin, mid), F32)),
        (both, partner(both, 1)),
        moved=2_000_000,
        last=True,
    )
    return (
        input_grad.reshape(volume.shape),
        jnp.transpose(mid_grad.reshape(27, cin, mid), (2, 0, 1)),
        jnp.transpose(top_grad.reshape(27, mid, cout), (2, 0, 1)),
    )


def solution(mesh):
    return jax.shard_map(
        shards,
        mesh=mesh,
        in_specs=(P(None, "spatial", "groups", None), P(), P(), P(None, "spatial", "groups", None)),
        out_specs=(
            P(None, "spatial", "groups", None),
            P("groups", None, None),
            P("groups", None, None),
        ),
        check_vma=False,
    )
```

```python
import math

import jax
import jax.numpy as jnp
from jax import lax
from jax.experimental import pallas as pl
from jax.experimental.pallas import tpu as pltpu
from jax.sharding import PartitionSpec as P

BF16 = jnp.bfloat16
F32 = jnp.float32
ROOT = math.sqrt(2.0 / math.pi)
CUBIC = 0.044715
THREE = (0, 1, 2)
VMEM_LIMIT = 20 << 20


def kernel_call(body, name, outs, args, scratch=(), flops=0, moved=0, last=False):
    whole = pl.BlockSpec(memory_space=pltpu.VMEM)
    args = [pltpu.with_memory_space_constraint(arg, pltpu.VMEM) for arg in args]
    if not last:
        outs = jax.tree.map(lambda out: pltpu.VMEM(out.shape, out.dtype), outs)
    return pl.pallas_call(
        body,
        name=name,
        out_shape=outs,
        in_specs=[whole] * len(args),
        out_specs=jax.tree.map(lambda _: whole, outs),
        scratch_shapes=list(scratch),
        compiler_params=pltpu.CompilerParams(vmem_limit_bytes=VMEM_LIMIT),
        cost_estimate=pl.CostEstimate(flops=flops, bytes_accessed=moved, transcendentals=0),
    )(*args)


def dot(a, b, contract=((1,), (0,))):
    return lax.dot_general(a, b, (contract, ((), ())), preferred_element_type=F32)


def parity_matrix(width, inverse):
    first = lax.broadcasted_iota(jnp.int32, (width, width), 0)
    second = lax.broadcasted_iota(jnp.int32, (width, width), 1)
    cell, slot = (second, first) if inverse else (first, second)
    half = width // 2
    source = jnp.where(slot < half, 2 * slot, 2 * (slot - half) + 1)
    return (cell == source).astype(F32).astype(BF16)


def later(row):
    lane = lax.broadcasted_iota(jnp.int32, row.shape, 1)
    return jnp.where(lane == 0, 0.0, pltpu.roll(row, 1, 1))


def earlier(row):
    lane = lax.broadcasted_iota(jnp.int32, row.shape, 1)
    last = row.shape[1] - 1
    return jnp.where(lane == last, 0.0, pltpu.roll(row, last, 1))


def gelu(value):
    return (0.5 * value) * (1.0 + jnp.tanh(value * (ROOT + ROOT * CUBIC * (value * value))))


def gelu_slope(value):
    square = value * value
    tanh = jnp.tanh(value * (ROOT + ROOT * CUBIC * square))
    inner = 0.5 * ROOT + 1.5 * ROOT * CUBIC * square
    return 0.5 + 0.5 * tanh + value * inner * (1.0 - tanh * tanh)


def sort_plane(rows, split, store, h, w):
    channels = rows[0].shape[0]
    done = dot(jnp.concatenate(rows, axis=0), split).astype(BF16)
    store(0, jnp.zeros((channels, w), BF16))
    store(h + 1, jnp.zeros((channels, w), BF16))
    for y in range(h):
        store(y + 1, done[y * channels : (y + 1) * channels])


def lanes(start, size):
    return pl.ds(pl.multiple_of(start, 128), size)


def middle_planes(vol_ref, wmid_ref, pre_ref, begin, count, h, w, emit):
    half = w // 2
    mid = pre_ref.shape[0]
    for pz in range(count // 2):
        sums = [None] * (h // 2)
        for j in (2 * pz, 2 * pz + 1):
            at = (begin + j) * (h + 2) * w
            cols = jnp.concatenate([vol_ref[:, lanes(at + (a * (h + 2) + b) * w, h * w)] for a in THREE for b in THREE], axis=0)
            part = dot(wmid_ref[...], cols)
            for y in range(h):
                even = slice(y * w, y * w + half)
                odd = slice(y * w + half, (y + 1) * w)
                pre_even = part[mid : 2 * mid, even] + later(part[:mid, odd]) + part[2 * mid :, odd]
                pre_odd = part[mid : 2 * mid, odd] + part[:mid, even] + earlier(part[2 * mid :, even])
                out = (j * h + y) * w
                pre_ref[:, out : out + half] = pre_even
                pre_ref[:, out + half : out + w] = pre_odd
                both = gelu(pre_even) + gelu(pre_odd)
                sums[y // 2] = both if sums[y // 2] is None else sums[y // 2] + both
        emit(pz, [row * 0.125 for row in sums])


def pool_rows(pool_ref, base, rows, outside):
    mid, half = rows[0].shape
    zero = jnp.zeros((3 * mid, half), BF16)
    pool_ref[:, lanes(base, half)] = zero
    pool_ref[:, lanes(base + (len(rows) + 1) * half, half)] = zero
    for y, row in enumerate(rows):
        row = jnp.where(outside, 0.0, row).astype(BF16)
        wide = row.astype(F32)
        at = lanes(base + (y + 1) * half, half)
        pool_ref[:mid, at] = later(wide).astype(BF16)
        pool_ref[mid : 2 * mid, at] = row
        pool_ref[2 * mid :, at] = earlier(wide).astype(BF16)


def near_kernel(near_ref, own_ref, wmid_ref, vol_ref, pre_ref, pool_ref, *, h, w, spatial):
    here = lax.axis_index("spatial")
    core = here % 2
    split = parity_matrix(w, False)
    size = (h + 2) * w
    halo = near_ref.shape[1] // (h * w)
    own = own_ref.shape[1] // (h * w)
    for ref, count, start in ((own_ref, own, core * halo), (near_ref, halo, (1 - core) * own)):
        for z in range(count):
            rows = [ref[:, (z * h + y) * w : (z * h + y + 1) * w] for y in range(h)]

            def store(row, value, at=(start + z) * size):
                vol_ref[:, lanes(at + row * w, w)] = value

            sort_plane(rows, split, store, h, w)
    count = pre_ref.shape[1] // (h * w)
    pooled = count // 2
    prow = pool_ref.shape[1] // pooled

    def emit(pz, rows):
        first = (core == 1) & (here == 0) if pz == 0 else False
        last = (core == 0) & (here == spatial - 1) if pz == pooled - 1 else False
        pool_rows(pool_ref, pz * prow, rows, jnp.logical_or(first, last))

    middle_planes(vol_ref, wmid_ref, pre_ref, 1 - core, count, h, w, emit)


def far_kernel(
    far_ref, vol_near_ref, pool_near_ref, wmid_ref, wtop_ref, cot_ref, delta_ref, pre_ref, vol_ref, pool_ref, *, h, w, spatial
):
    half = w // 2
    here = lax.axis_index("spatial")
    core = here % 2
    split = parity_matrix(w, False)
    size = (h + 2) * w
    halo = far_ref.shape[1] // (h * w)
    known = vol_near_ref.shape[1]
    vol_ref[:, lanes((1 - core) * halo * size, known)] = vol_near_ref[...]
    for z in range(halo):
        rows = [far_ref[:, (z * h + y) * w : (z * h + y + 1) * w] for y in range(h)]

        def store(row, value, at=core * known + z * size):
            vol_ref[:, lanes(at + row * w, w)] = value

        sort_plane(rows, split, store, h, w)
    count = pre_ref.shape[1] // (h * w)
    pooled = count // 2
    hp = h // 2
    prow = (hp + 2) * half
    pool_ref[:, lanes((1 - core) * pooled * prow, pooled * prow)] = pool_near_ref[...]

    def emit(pz, rows):
        first = (core == 0) & (here == 0) if pz == 0 else False
        last = (core == 1) & (here == spatial - 1) if pz == pooled - 1 else False
        pool_rows(pool_ref, (core * pooled + pz) * prow, rows, jnp.logical_or(first, last))

    middle_planes(vol_ref, wmid_ref, pre_ref, core * count, count, h, w, emit)
    for j in range(delta_ref.shape[1] // (hp * half)):
        cols = jnp.concatenate(
            [pool_ref[:, (j + a) * prow + b * half : (j + a) * prow + (b + hp) * half] for a in THREE for b in THREE], axis=0
        )
        pre_top = dot(wtop_ref[...], cols, ((0,), (0,)))
        at = slice(j * hp * half, (j + 1) * hp * half)
        delta_ref[:, at] = (cot_ref[:, at].astype(F32) * gelu_slope(pre_top)).astype(BF16)


def halve(whole_ref, keep_ref, send_ref):
    core = lax.axis_index("spatial") % 2
    rows = keep_ref.shape[0]
    keep_ref[...] = whole_ref[pl.ds(pl.multiple_of(core * rows, 16), rows), :]
    sent = whole_ref[pl.ds(pl.multiple_of((1 - core) * rows, 16), rows), :].astype(BF16)
    send_ref[send_ref.shape[0] - rows :, :] = sent


def slope_kernel(near_ref, far_ref, slope_ref, *, plane):
    core = lax.axis_index("spatial") % 2
    part = slope_ref.shape[1] // 2
    for ref, side in ((near_ref, 1 - core), (far_ref, core)):
        for at in range(0, part, 128):
            value = 0.125 * gelu_slope(ref[:, lanes((1 - side) * plane + at, 128)])
            slope_ref[:, lanes(side * part + at, 128)] = value


def top_kernel(delta_ref, pool_ref, keep_ref, send_ref, out_ref, *, hp, wp):
    cout = delta_ref.shape[0]
    for at in range(0, delta_ref.shape[1], wp):
        send_ref[at // wp * cout : (at // wp + 1) * cout, :] = delta_ref[:, at : at + wp]
    prow = (hp + 2) * wp
    planes = delta_ref.shape[1] // (hp * wp)
    for a in THREE:
        for b in THREE:
            block = jnp.concatenate(
                [pool_ref[:, (j + a) * prow + b * wp : (j + a) * prow + (b + hp) * wp] for j in range(planes)], axis=1
            )
            rows = slice((3 * a + b) * block.shape[0], (3 * a + b + 1) * block.shape[0])
            out_ref[rows, :] = dot(block, delta_ref[...], ((1,), (1,)))
    halve(out_ref, keep_ref, send_ref)


def backward_side(side, neighbour, own_ref, slope_ref, vol_ref, wtop_ref, field_ref, field_base, top_ref, shift_ref, h, w, spatial):
    half, hp = w // 2, h // 2
    here = lax.axis_index("spatial")
    trow = (hp + 2) * half
    depth = own_ref.shape[1] // (hp * half)
    zero = jnp.zeros((top_ref.shape[0], half), BF16)
    for z in range(depth):
        near_plane = neighbour(z)
        own_plane = own_ref[:, z * hp * half : (z + 1) * hp * half]
        for plane, base in ((own_plane, (1 - side) * depth * trow), (near_plane, side * depth * trow)):
            base = base + z * trow
            top_ref[:, lanes(base, half)] = zero
            top_ref[:, lanes(base + half, hp * half)] = plane
            top_ref[:, lanes(base + (hp + 1) * half, half)] = zero
    mid = slope_ref.shape[0]
    weights = jnp.concatenate(
        [
            jnp.concatenate([wtop_ref[(3 * ab + c) * mid : (3 * ab + c + 1) * mid, :] for ab in range(9)], axis=1)
            for c in THREE
        ],
        axis=0,
    )
    count = 2 * depth - 2
    cols = jnp.concatenate(
        [
            jnp.concatenate(
                [
                    top_ref[:, (j + 2 - a) * trow + (2 - b) * half : (j + 2 - a) * trow + (2 - b + hp) * half]
                    for j in range(count)
                ],
                axis=1,
            )
            for a in THREE
            for b in THREE
        ],
        axis=0,
    )
    part = dot(weights, cols)
    pools = []
    for k in range(count * hp):
        at = slice(k * half, (k + 1) * half)
        pools.append(part[mid : 2 * mid, at] + later(part[2 * mid :, at]) + earlier(part[:mid, at]))
    size = (h + 2) * w
    field_zero = jnp.zeros((mid, w), BF16)
    planes = 2 * count - 1
    for k in range(planes):
        base = field_base + k * size
        field_ref[:, lanes(base, w)] = field_zero
        field_ref[:, lanes(base + (h + 1) * w, w)] = field_zero
        for y in range(h):
            pool = jnp.where(side == 1, pools[k // 2 * hp + y // 2], pools[(k + 1) // 2 * hp + y // 2])
            if k == 0:
                pool = jnp.where((side == 0) & (here == 0), 0.0, pool)
            if k == planes - 1:
                pool = jnp.where((side == 1) & (here == spatial - 1), 0.0, pool)
            row = (k * h + y) * w
            at = side * planes * h * w + row
            even = (slope_ref[:, lanes(at, half)] * pool).astype(BF16)
            odd = (slope_ref[:, lanes(at + half, half)] * pool).astype(BF16)
            to = base + (y + 1) * w
            field_ref[:, lanes(to, half)] = even
            field_ref[:, lanes(to + half, half)] = odd
            shift_ref[:mid, row : row + half] = odd
            shift_ref[:mid, row + half : row + w] = earlier(even.astype(F32)).astype(BF16)
            shift_ref[mid : 2 * mid, row : row + half] = even
            shift_ref[mid : 2 * mid, row + half : row + w] = odd
            shift_ref[2 * mid :, row : row + half] = later(odd.astype(F32)).astype(BF16)
            shift_ref[2 * mid :, row + half : row + w] = even
    total = None
    for z in range(depth):
        at = (side * depth + z + 2) * size
        piece = jnp.concatenate([vol_ref[:, lanes(at + a * size + b * w, h * w)] for a in THREE for b in THREE], axis=0)
        moved = shift_ref[:, lanes((1 - side + z) * h * w, h * w)]
        product = dot(piece, moved, ((1,), (1,)))
        total = product if total is None else total + product
    return total


def backward_near_kernel(
    near_ref, own_ref, slope_ref, vol_ref, wtop_ref, part_ref, field_ref, top_ref, shift_ref, *, h, w, spatial
):
    core = lax.axis_index("spatial") % 2
    hp = h // 2
    cout = own_ref.shape[0]

    def neighbour(z):
        return jnp.concatenate([near_ref[k * cout : (k + 1) * cout, :] for k in range(z * hp, (z + 1) * hp)], axis=1)

    part_ref[...] = backward_side(
        1 - core, neighbour, own_ref, slope_ref, vol_ref, wtop_ref, field_ref, 0, top_ref, shift_ref, h, w, spatial
    )


def backward_far_kernel(
    far_ref, own_ref, slope_ref, vol_ref, wtop_ref, part_ref, field_near_ref, keep_ref, send_ref, field_ref, top_ref, shift_ref,
    mid_ref, *, h, w, spatial
):
    core = lax.axis_index("spatial") % 2
    size = h // 2 * (w // 2)
    known = field_near_ref.shape[1]
    field_ref[:, lanes((1 - core) * known, known)] = field_near_ref[...]

    def neighbour(z):
        return far_ref[:, z * size : (z + 1) * size]

    total = part_ref[...] + backward_side(
        core, neighbour, own_ref, slope_ref, vol_ref, wtop_ref, field_ref, core * known, top_ref, shift_ref, h, w, spatial
    )
    mid = field_ref.shape[0]
    rows = total.shape[0]
    half_rows = rows // 2
    mid_ref[:rows, :] = total[:, : 2 * mid]
    last = total[:, 2 * mid :]
    mid_ref[rows : rows + half_rows, :] = jnp.concatenate([last[:half_rows], last[half_rows:]], axis=1)
    spare = mid_ref.shape[0] - rows - half_rows
    if spare:
        mid_ref[rows + half_rows :, :] = jnp.zeros((spare, 2 * mid), F32)
    halve(mid_ref, keep_ref, send_ref)


def input_kernel(field_ref, wback_ref, out_ref, *, h, w):
    half = w // 2
    vrows = h + 2
    join = parity_matrix(w, True)
    ch = out_ref.shape[0]
    for z in range(out_ref.shape[1] // (h * w)):
        cols = jnp.concatenate(
            [
                field_ref[:, ((z + 2 - a) * vrows + 2 - b) * w : ((z + 2 - a) * vrows + 2 - b + h) * w]
                for a in THREE
                for b in THREE
            ],
            axis=0,
        )
        part = dot(wback_ref[...], cols)
        rows = []
        for y in range(h):
            even = slice(y * w, y * w + half)
            odd = slice(y * w + half, (y + 1) * w)
            grad_even = part[ch : 2 * ch, even] + later(part[2 * ch :, odd]) + part[:ch, odd]
            grad_odd = part[ch : 2 * ch, odd] + part[2 * ch :, even] + earlier(part[:ch, even])
            rows.append(jnp.concatenate([grad_even, grad_odd], axis=1).astype(BF16))
        joined = dot(jnp.concatenate(rows, axis=0), join).astype(BF16)
        for y in range(h):
            out_ref[:, (z * h + y) * w : (z * h + y + 1) * w] = joined[y * ch : (y + 1) * ch]


def finish_kernel(own_ref, other_ref, top_ref, mid_ref, *, scale_top, scale_mid):
    core = lax.axis_index("spatial") % 2
    top_rows = top_ref.shape[0] // 2
    top_ref[pl.ds(pl.multiple_of(core * top_rows, 16), top_rows), :] = own_ref[:top_rows].astype(F32) * scale_top
    top_ref[pl.ds(pl.multiple_of((1 - core) * top_rows, 16), top_rows), :] = other_ref[:top_rows].astype(F32) * scale_top
    mid_rows = (own_ref.shape[0] - top_rows) // 2
    own = own_ref[top_rows : top_rows + mid_rows].astype(F32) + own_ref[top_rows + mid_rows :].astype(F32)
    other = other_ref[top_rows : top_rows + mid_rows].astype(F32) + other_ref[top_rows + mid_rows :].astype(F32)
    low = jnp.where(core == 0, own, other)
    high = jnp.where(core == 0, other, own)
    whole = jnp.concatenate([low, high], axis=0) * scale_mid
    rows = mid_ref.shape[0] // 3
    mid = mid_ref.shape[1]
    q = rows // 9
    for ab in range(9):
        block = whole[ab * q : (ab + 1) * q]
        mid_ref[(3 * ab) * q : (3 * ab + 1) * q, :] = block[:, :mid]
        mid_ref[(3 * ab + 1) * q : (3 * ab + 2) * q, :] = block[:, mid:]
    half_rows = rows // 2
    last = whole[rows : rows + half_rows]
    last = jnp.concatenate([last[:, :mid], last[:, mid:]], axis=0)
    for ab in range(9):
        mid_ref[(3 * ab + 2) * q : (3 * ab + 3) * q, :] = last[ab * q : (ab + 1) * q]


def partner(block, bit):
    size = lax.axis_size("spatial")
    return lax.ppermute(block, "spatial", [(i, i ^ bit) for i in range(size)])


def across(block):
    size = lax.axis_size("spatial")
    pairs = [(i, i + 1) for i in range(1, size - 1, 2)]
    return lax.ppermute(block, "spatial", pairs + [(j, i) for i, j in pairs])


def bit_is_clear(bit):
    return (lax.axis_index("spatial") & bit) == 0


def rounded(block):
    return lax.optimization_barrier(block.astype(BF16))


def add_both(sent, bit):
    return sent.astype(F32) + partner(sent, bit).astype(F32)


def halves(block, low):
    rows = block.shape[0] // 2
    mine = jnp.where(low, block[:rows], block[rows:])
    other = jnp.where(low, block[rows:], block[:rows])
    return mine, rounded(other)


def in_order(block, other, low):
    return jnp.where(low, block, other), jnp.where(low, other, block)


def far_bits():
    return [1 << k for k in range(2, lax.axis_size("spatial").bit_length() - 1)]


def shards(volume, weights_mid, weights_top, cotangent):
    spatial = lax.axis_size("spatial")
    cin, nz, h, w = volume.shape
    mid = weights_mid.shape[0]
    cout, nzp, hp, wp = cotangent.shape
    shape = jax.ShapeDtypeStruct
    plane = h * w
    volume, first_core, low = lax.optimization_barrier((volume, bit_is_clear(1), bit_is_clear(4)))
    flat = volume.reshape(cin, nz * plane)
    early, late = flat[:, : (nz - 1) * plane], flat[:, plane:]
    far = across(jnp.where(first_core, early, late))
    near = partner(jnp.where(first_core, late, early), 1)
    split = weights_mid.reshape(mid, 9, 3, cin)
    wmid = jnp.transpose(split, (2, 0, 1, 3)).reshape(3 * mid, 9 * cin)
    wback = jnp.transpose(split, (2, 3, 1, 0)).reshape(3 * cin, 9 * mid)
    wtop = jnp.transpose(weights_top, (1, 2, 0)).reshape(27 * mid, cout)
    cot = cotangent.reshape(cout, nzp * hp * wp)
    size = (h + 2) * w
    count = nz // 2 + 2
    halo = nz - 1
    pool_size = (hp + 2) * wp
    vol_near, pre_near, pool_near = kernel_call(
        lambda *refs: near_kernel(*refs, h=h, w=w, spatial=spatial),
        "near_side",
        (
            shape((cin, (nz + halo) * size), BF16),
            shape((mid, count * plane), F32),
            shape((3 * mid, count // 2 * pool_size), BF16),
        ),
        (near, flat, wmid),
        flops=900_000_000,
        moved=3_000_000,
    )
    far, wback, vol_near, pool_near = lax.optimization_barrier((far, wback, vol_near, pool_near))
    delta, pre_far, vol, pool = kernel_call(
        lambda *refs: far_kernel(*refs, h=h, w=w, spatial=spatial),
        "far_side",
        (
            shape(cot.shape, BF16),
            shape((mid, count * plane), F32),
            shape((cin, (nz + 2 * halo) * size), BF16),
            shape((3 * mid, count * pool_size), BF16),
        ),
        (far, vol_near, pool_near, wmid, wtop, cot),
        flops=900_000_000,
        moved=4_000_000,
    )
    delta_far = across(delta)
    top_rows = 27 * mid
    delta_rows = delta.size // cout
    keep, send = kernel_call(
        lambda *refs: top_kernel(*refs, hp=hp, wp=wp),
        "top_part",
        (shape((top_rows // 2, cout), F32), shape((delta_rows + top_rows // 2, cout), BF16)),
        (delta, pool),
        scratch=(pltpu.VMEM((top_rows, cout), F32),),
        flops=226_000_000,
        moved=1_500_000,
    )
    slope = kernel_call(
        lambda *refs: slope_kernel(*refs, plane=plane),
        "slope",
        shape((mid, (nz + 2) * plane), F32),
        (pre_near, pre_far),
        flops=100_000_000,
        moved=3_000_000,
    )
    delta_near = partner(send, 1)
    mine, other = halves(keep + delta_near[delta_rows:].astype(F32), low)
    top_received = partner(other, 4)
    mid_rows = -(-27 * cin // 64) * 16
    side_scratch = (
        pltpu.VMEM((cout, 2 * nzp * (hp + 2) * wp), BF16),
        pltpu.VMEM((3 * mid, (nz // 2 + 1) * plane), BF16),
    )
    part, field_near = kernel_call(
        lambda *refs: backward_near_kernel(*refs, h=h, w=w, spatial=spatial),
        "backward_near",
        (shape((9 * cin, 3 * mid), F32), shape((mid, (nz // 2 + 1) * size), BF16)),
        (delta_near, delta, slope, vol, wtop),
        scratch=side_scratch,
        flops=500_000_000,
        moved=3_000_000,
    )
    delta_far, part, field_near = lax.optimization_barrier((delta_far, part, field_near))
    keep, send, field = kernel_call(
        lambda *refs: backward_far_kernel(*refs, h=h, w=w, spatial=spatial),
        "backward_far",
        (
            shape((mid_rows, 2 * mid), F32),
            shape((mid_rows, 2 * mid), BF16),
            shape((mid, (nz + 2) * size), BF16),
        ),
        (delta_far, delta, slope, vol, wtop, part, field_near),
        scratch=side_scratch + (pltpu.VMEM((2 * mid_rows, 2 * mid), F32),),
        flops=500_000_000,
        moved=4_000_000,
    )
    keep, send, mine, top_received = lax.optimization_barrier((keep, send, mine, top_received))
    top_sum = rounded(mine + top_received.astype(F32))
    bits = far_bits()[1:]
    top_sum, send = lax.optimization_barrier((top_sum, send))
    for bit in bits:
        top_sum = rounded(add_both(top_sum, bit))
    mid_sum = rounded(keep + partner(send, 1).astype(F32))
    mid_sum = rounded(add_both(mid_sum, 2))
    top_sum, mid_sum = lax.optimization_barrier((top_sum, mid_sum))
    mid_sum, field = lax.optimization_barrier((mid_sum, field))
    for bit in bits:
        mid_sum = rounded(add_both(mid_sum, bit))
    top_sum = rounded(add_both(top_sum, 2))
    input_grad = kernel_call(
        lambda *refs: input_kernel(*refs, h=h, w=w),
        "input_grad",
        shape((cin, nz * plane), BF16),
        (field, wback),
        flops=452_000_000,
        moved=2_000_000,
    )
    both = jnp.concatenate([top_sum, mid_sum], axis=0)
    both, input_grad = lax.optimization_barrier((both, input_grad))
    received = partner(both, 4)
    top_sum = jnp.concatenate(in_order(top_sum, received[: top_sum.shape[0]], low), axis=0)
    mid_sum = mid_sum.astype(F32) + received[-mid_rows:].astype(F32)
    mid_high = rounded(mid_sum)
    mid_low = rounded(mid_sum - mid_high.astype(F32))
    both = jnp.concatenate([top_sum, mid_high, mid_low], axis=0)
    top_grad, mid_grad = kernel_call(
        lambda *refs: finish_kernel(
            *refs,
            scale_top=1.0 / math.sqrt(nzp * hp * wp * spatial),
            scale_mid=1.0 / math.sqrt(nz * plane * spatial),
        ),
        "finish",
        (shape((27 * mid, cout), F32), shape((27 * cin, mid), F32)),
        (both, partner(both, 1)),
        moved=2_000_000,
        last=True,
    )
    return (
        input_grad.reshape(volume.shape),
        jnp.transpose(mid_grad.reshape(27, cin, mid), (2, 0, 1)),
        jnp.transpose(top_grad.reshape(27, mid, cout), (2, 0, 1)),
    )


def solution(mesh):
    return jax.shard_map(
        shards,
        mesh=mesh,
        in_specs=(P(None, "spatial", "groups", None), P(), P(), P(None, "spatial", "groups", None)),
        out_specs=(
            P(None, "spatial", "groups", None),
            P("groups", None, None),
            P("groups", None, None),
        ),
        check_vma=False,
    )
```

```python
import math

import jax
import jax.numpy as jnp
from jax import lax
from jax.experimental import pallas as pl
from jax.experimental.pallas import tpu as pltpu
from jax.sharding import PartitionSpec as P

BF16 = jnp.bfloat16
F32 = jnp.float32
ROOT = math.sqrt(2.0 / math.pi)
CUBIC = 0.044715
THREE = (0, 1, 2)
VMEM_LIMIT = 20 << 20


def kernel_call(body, name, outs, args, scratch=(), flops=0, moved=0, last=False):
    whole = pl.BlockSpec(memory_space=pltpu.VMEM)
    args = [pltpu.with_memory_space_constraint(arg, pltpu.VMEM) for arg in args]
    if not last:
        outs = jax.tree.map(lambda out: pltpu.VMEM(out.shape, out.dtype), outs)
    return pl.pallas_call(
        body,
        name=name,
        out_shape=outs,
        in_specs=[whole] * len(args),
        out_specs=jax.tree.map(lambda _: whole, outs),
        scratch_shapes=list(scratch),
        compiler_params=pltpu.CompilerParams(vmem_limit_bytes=VMEM_LIMIT),
        cost_estimate=pl.CostEstimate(flops=flops, bytes_accessed=moved, transcendentals=0),
    )(*args)


def dot(a, b, contract=((1,), (0,))):
    return lax.dot_general(a, b, (contract, ((), ())), preferred_element_type=F32)


def parity_matrix(width, inverse):
    first = lax.broadcasted_iota(jnp.int32, (width, width), 0)
    second = lax.broadcasted_iota(jnp.int32, (width, width), 1)
    cell, slot = (second, first) if inverse else (first, second)
    half = width // 2
    source = jnp.where(slot < half, 2 * slot, 2 * (slot - half) + 1)
    return (cell == source).astype(F32).astype(BF16)


def later(row):
    lane = lax.broadcasted_iota(jnp.int32, row.shape, 1)
    return jnp.where(lane == 0, 0.0, pltpu.roll(row, 1, 1))


def earlier(row):
    lane = lax.broadcasted_iota(jnp.int32, row.shape, 1)
    last = row.shape[1] - 1
    return jnp.where(lane == last, 0.0, pltpu.roll(row, last, 1))


def gelu(value):
    return (0.5 * value) * (1.0 + jnp.tanh(value * (ROOT + ROOT * CUBIC * (value * value))))


def gelu_slope(value):
    square = value * value
    tanh = jnp.tanh(value * (ROOT + ROOT * CUBIC * square))
    inner = 0.5 * ROOT + 1.5 * ROOT * CUBIC * square
    return 0.5 + 0.5 * tanh + value * inner * (1.0 - tanh * tanh)


def sort_plane(rows, split, store, h, w):
    channels = rows[0].shape[0]
    done = dot(jnp.concatenate(rows, axis=0), split).astype(BF16)
    store(0, jnp.zeros((channels, w), BF16))
    store(h + 1, jnp.zeros((channels, w), BF16))
    for y in range(h):
        store(y + 1, done[y * channels : (y + 1) * channels])


def lanes(start, size):
    return pl.ds(pl.multiple_of(start, 128), size)


def middle_planes(vol_ref, wmid_ref, pre_ref, begin, count, h, w, emit):
    half = w // 2
    mid = pre_ref.shape[0]
    for pz in range(count // 2):
        sums = [None] * (h // 2)
        for j in (2 * pz, 2 * pz + 1):
            at = (begin + j) * (h + 2) * w
            cols = jnp.concatenate([vol_ref[:, lanes(at + (a * (h + 2) + b) * w, h * w)] for a in THREE for b in THREE], axis=0)
            part = dot(wmid_ref[...], cols)
            for y in range(h):
                even = slice(y * w, y * w + half)
                odd = slice(y * w + half, (y + 1) * w)
                pre_even = part[mid : 2 * mid, even] + later(part[:mid, odd]) + part[2 * mid :, odd]
                pre_odd = part[mid : 2 * mid, odd] + part[:mid, even] + earlier(part[2 * mid :, even])
                out = (j * h + y) * w
                pre_ref[:, out : out + half] = pre_even
                pre_ref[:, out + half : out + w] = pre_odd
                both = gelu(pre_even) + gelu(pre_odd)
                sums[y // 2] = both if sums[y // 2] is None else sums[y // 2] + both
        emit(pz, [row * 0.125 for row in sums])


def pool_rows(pool_ref, base, rows, outside):
    mid, half = rows[0].shape
    zero = jnp.zeros((3 * mid, half), BF16)
    pool_ref[:, lanes(base, half)] = zero
    pool_ref[:, lanes(base + (len(rows) + 1) * half, half)] = zero
    for y, row in enumerate(rows):
        row = jnp.where(outside, 0.0, row).astype(BF16)
        wide = row.astype(F32)
        at = lanes(base + (y + 1) * half, half)
        pool_ref[:mid, at] = later(wide).astype(BF16)
        pool_ref[mid : 2 * mid, at] = row
        pool_ref[2 * mid :, at] = earlier(wide).astype(BF16)


def near_kernel(near_ref, own_ref, wmid_ref, vol_ref, pre_ref, pool_ref, *, h, w, spatial):
    here = lax.axis_index("spatial")
    core = here % 2
    split = parity_matrix(w, False)
    size = (h + 2) * w
    halo = near_ref.shape[1] // (h * w)
    own = own_ref.shape[1] // (h * w)
    for ref, count, start in ((own_ref, own, core * halo), (near_ref, halo, (1 - core) * own)):
        for z in range(count):
            rows = [ref[:, (z * h + y) * w : (z * h + y + 1) * w] for y in range(h)]

            def store(row, value, at=(start + z) * size):
                vol_ref[:, lanes(at + row * w, w)] = value

            sort_plane(rows, split, store, h, w)
    count = pre_ref.shape[1] // (h * w)
    pooled = count // 2
    prow = pool_ref.shape[1] // pooled

    def emit(pz, rows):
        first = (core == 1) & (here == 0) if pz == 0 else False
        last = (core == 0) & (here == spatial - 1) if pz == pooled - 1 else False
        pool_rows(pool_ref, pz * prow, rows, jnp.logical_or(first, last))

    middle_planes(vol_ref, wmid_ref, pre_ref, 1 - core, count, h, w, emit)


def far_kernel(
    far_ref, vol_near_ref, pool_near_ref, wmid_ref, wtop_ref, cot_ref, delta_ref, pre_ref, vol_ref, keep_ref, send_ref, pool_ref,
    grad_ref, *, h, w, spatial
):
    half = w // 2
    here = lax.axis_index("spatial")
    core = here % 2
    split = parity_matrix(w, False)
    size = (h + 2) * w
    halo = far_ref.shape[1] // (h * w)
    known = vol_near_ref.shape[1]
    vol_ref[:, lanes((1 - core) * halo * size, known)] = vol_near_ref[...]
    for z in range(halo):
        rows = [far_ref[:, (z * h + y) * w : (z * h + y + 1) * w] for y in range(h)]

        def store(row, value, at=core * known + z * size):
            vol_ref[:, lanes(at + row * w, w)] = value

        sort_plane(rows, split, store, h, w)
    count = pre_ref.shape[1] // (h * w)
    pooled = count // 2
    hp = h // 2
    prow = (hp + 2) * half
    pool_ref[:, lanes((1 - core) * pooled * prow, pooled * prow)] = pool_near_ref[...]

    def emit(pz, rows):
        first = (core == 0) & (here == 0) if pz == 0 else False
        last = (core == 1) & (here == spatial - 1) if pz == pooled - 1 else False
        pool_rows(pool_ref, (core * pooled + pz) * prow, rows, jnp.logical_or(first, last))

    middle_planes(vol_ref, wmid_ref, pre_ref, core * count, count, h, w, emit)
    for j in range(delta_ref.shape[1] // (hp * half)):
        cols = jnp.concatenate(
            [pool_ref[:, (j + a) * prow + b * half : (j + a) * prow + (b + hp) * half] for a in THREE for b in THREE], axis=0
        )
        pre_top = dot(wtop_ref[...], cols, ((0,), (0,)))
        at = slice(j * hp * half, (j + 1) * hp * half)
        delta_ref[:, at] = (cot_ref[:, at].astype(F32) * gelu_slope(pre_top)).astype(BF16)
    top_part(delta_ref, pool_ref, keep_ref, send_ref, grad_ref, hp, half)


def halve(whole_ref, keep_ref, send_ref):
    core = lax.axis_index("spatial") % 2
    rows = keep_ref.shape[0]
    keep_ref[...] = whole_ref[pl.ds(pl.multiple_of(core * rows, 16), rows), :]
    sent = whole_ref[pl.ds(pl.multiple_of((1 - core) * rows, 16), rows), :].astype(BF16)
    send_ref[send_ref.shape[0] - rows :, :] = sent


def slope_kernel(near_ref, far_ref, slope_ref, *, plane):
    core = lax.axis_index("spatial") % 2
    part = slope_ref.shape[1] // 2
    for ref, side in ((near_ref, 1 - core), (far_ref, core)):
        for at in range(0, part, 128):
            value = 0.125 * gelu_slope(ref[:, lanes((1 - side) * plane + at, 128)])
            slope_ref[:, lanes(side * part + at, 128)] = value


def top_part(delta_ref, pool_ref, keep_ref, send_ref, out_ref, hp, wp):
    cout = delta_ref.shape[0]
    for at in range(0, delta_ref.shape[1], wp):
        send_ref[at // wp * cout : (at // wp + 1) * cout, :] = delta_ref[:, at : at + wp]
    prow = (hp + 2) * wp
    planes = delta_ref.shape[1] // (hp * wp)
    for a in THREE:
        for b in THREE:
            block = jnp.concatenate(
                [pool_ref[:, (j + a) * prow + b * wp : (j + a) * prow + (b + hp) * wp] for j in range(planes)], axis=1
            )
            rows = slice((3 * a + b) * block.shape[0], (3 * a + b + 1) * block.shape[0])
            out_ref[rows, :] = dot(block, delta_ref[...], ((1,), (1,)))
    halve(out_ref, keep_ref, send_ref)


def backward_side(side, neighbour, own_ref, slope_ref, vol_ref, wtop_ref, field_ref, field_base, top_ref, shift_ref, h, w, spatial):
    half, hp = w // 2, h // 2
    here = lax.axis_index("spatial")
    trow = (hp + 2) * half
    depth = own_ref.shape[1] // (hp * half)
    zero = jnp.zeros((top_ref.shape[0], half), BF16)
    for z in range(depth):
        near_plane = neighbour(z)
        own_plane = own_ref[:, z * hp * half : (z + 1) * hp * half]
        for plane, base in ((own_plane, (1 - side) * depth * trow), (near_plane, side * depth * trow)):
            base = base + z * trow
            top_ref[:, lanes(base, half)] = zero
            top_ref[:, lanes(base + half, hp * half)] = plane
            top_ref[:, lanes(base + (hp + 1) * half, half)] = zero
    mid = slope_ref.shape[0]
    weights = jnp.concatenate(
        [
            jnp.concatenate([wtop_ref[(3 * ab + c) * mid : (3 * ab + c + 1) * mid, :] for ab in range(9)], axis=1)
            for c in THREE
        ],
        axis=0,
    )
    count = 2 * depth - 2
    cols = jnp.concatenate(
        [
            jnp.concatenate(
                [
                    top_ref[:, (j + 2 - a) * trow + (2 - b) * half : (j + 2 - a) * trow + (2 - b + hp) * half]
                    for j in range(count)
                ],
                axis=1,
            )
            for a in THREE
            for b in THREE
        ],
        axis=0,
    )
    part = dot(weights, cols)
    pools = []
    for k in range(count * hp):
        at = slice(k * half, (k + 1) * half)
        pools.append(part[mid : 2 * mid, at] + later(part[2 * mid :, at]) + earlier(part[:mid, at]))
    size = (h + 2) * w
    field_zero = jnp.zeros((mid, w), BF16)
    planes = 2 * count - 1
    for k in range(planes):
        base = field_base + k * size
        field_ref[:, lanes(base, w)] = field_zero
        field_ref[:, lanes(base + (h + 1) * w, w)] = field_zero
        for y in range(h):
            pool = jnp.where(side == 1, pools[k // 2 * hp + y // 2], pools[(k + 1) // 2 * hp + y // 2])
            if k == 0:
                pool = jnp.where((side == 0) & (here == 0), 0.0, pool)
            if k == planes - 1:
                pool = jnp.where((side == 1) & (here == spatial - 1), 0.0, pool)
            row = (k * h + y) * w
            at = side * planes * h * w + row
            even = (slope_ref[:, lanes(at, half)] * pool).astype(BF16)
            odd = (slope_ref[:, lanes(at + half, half)] * pool).astype(BF16)
            to = base + (y + 1) * w
            field_ref[:, lanes(to, half)] = even
            field_ref[:, lanes(to + half, half)] = odd
            shift_ref[:mid, row : row + half] = odd
            shift_ref[:mid, row + half : row + w] = earlier(even.astype(F32)).astype(BF16)
            shift_ref[mid : 2 * mid, row : row + half] = even
            shift_ref[mid : 2 * mid, row + half : row + w] = odd
            shift_ref[2 * mid :, row : row + half] = later(odd.astype(F32)).astype(BF16)
            shift_ref[2 * mid :, row + half : row + w] = even
    total = None
    for z in range(depth):
        at = (side * depth + z + 2) * size
        piece = jnp.concatenate([vol_ref[:, lanes(at + a * size + b * w, h * w)] for a in THREE for b in THREE], axis=0)
        moved = shift_ref[:, lanes((1 - side + z) * h * w, h * w)]
        product = dot(piece, moved, ((1,), (1,)))
        total = product if total is None else total + product
    return total


def backward_near_kernel(
    near_ref, own_ref, slope_ref, vol_ref, wtop_ref, part_ref, field_ref, top_ref, shift_ref, *, h, w, spatial
):
    core = lax.axis_index("spatial") % 2
    hp = h // 2
    cout = own_ref.shape[0]

    def neighbour(z):
        return jnp.concatenate([near_ref[k * cout : (k + 1) * cout, :] for k in range(z * hp, (z + 1) * hp)], axis=1)

    part_ref[...] = backward_side(
        1 - core, neighbour, own_ref, slope_ref, vol_ref, wtop_ref, field_ref, 0, top_ref, shift_ref, h, w, spatial
    )


def backward_far_kernel(
    far_ref, own_ref, slope_ref, vol_ref, wtop_ref, part_ref, field_near_ref, keep_ref, send_ref, field_ref, top_ref, shift_ref,
    mid_ref, *, h, w, spatial
):
    core = lax.axis_index("spatial") % 2
    size = h // 2 * (w // 2)
    known = field_near_ref.shape[1]
    field_ref[:, lanes((1 - core) * known, known)] = field_near_ref[...]

    def neighbour(z):
        return far_ref[:, z * size : (z + 1) * size]

    total = part_ref[...] + backward_side(
        core, neighbour, own_ref, slope_ref, vol_ref, wtop_ref, field_ref, core * known, top_ref, shift_ref, h, w, spatial
    )
    mid = field_ref.shape[0]
    rows = total.shape[0]
    half_rows = rows // 2
    mid_ref[:rows, :] = total[:, : 2 * mid]
    last = total[:, 2 * mid :]
    mid_ref[rows : rows + half_rows, :] = jnp.concatenate([last[:half_rows], last[half_rows:]], axis=1)
    spare = mid_ref.shape[0] - rows - half_rows
    if spare:
        mid_ref[rows + half_rows :, :] = jnp.zeros((spare, 2 * mid), F32)
    halve(mid_ref, keep_ref, send_ref)


def input_kernel(field_ref, wback_ref, out_ref, *, h, w):
    half = w // 2
    vrows = h + 2
    join = parity_matrix(w, True)
    ch = out_ref.shape[0]
    for z in range(out_ref.shape[1] // (h * w)):
        cols = jnp.concatenate(
            [
                field_ref[:, ((z + 2 - a) * vrows + 2 - b) * w : ((z + 2 - a) * vrows + 2 - b + h) * w]
                for a in THREE
                for b in THREE
            ],
            axis=0,
        )
        part = dot(wback_ref[...], cols)
        rows = []
        for y in range(h):
            even = slice(y * w, y * w + half)
            odd = slice(y * w + half, (y + 1) * w)
            grad_even = part[ch : 2 * ch, even] + later(part[2 * ch :, odd]) + part[:ch, odd]
            grad_odd = part[ch : 2 * ch, odd] + part[2 * ch :, even] + earlier(part[:ch, even])
            rows.append(jnp.concatenate([grad_even, grad_odd], axis=1).astype(BF16))
        joined = dot(jnp.concatenate(rows, axis=0), join).astype(BF16)
        for y in range(h):
            out_ref[:, (z * h + y) * w : (z * h + y + 1) * w] = joined[y * ch : (y + 1) * ch]


def finish_kernel(own_ref, other_ref, top_ref, mid_ref, *, scale_top, scale_mid):
    core = lax.axis_index("spatial") % 2
    top_rows = top_ref.shape[0] // 2
    top_ref[pl.ds(pl.multiple_of(core * top_rows, 16), top_rows), :] = own_ref[:top_rows].astype(F32) * scale_top
    top_ref[pl.ds(pl.multiple_of((1 - core) * top_rows, 16), top_rows), :] = other_ref[:top_rows].astype(F32) * scale_top
    mid_rows = (own_ref.shape[0] - top_rows) // 2
    own = own_ref[top_rows : top_rows + mid_rows].astype(F32) + own_ref[top_rows + mid_rows :].astype(F32)
    other = other_ref[top_rows : top_rows + mid_rows].astype(F32) + other_ref[top_rows + mid_rows :].astype(F32)
    low = jnp.where(core == 0, own, other)
    high = jnp.where(core == 0, other, own)
    whole = jnp.concatenate([low, high], axis=0) * scale_mid
    rows = mid_ref.shape[0] // 3
    mid = mid_ref.shape[1]
    q = rows // 9
    for ab in range(9):
        block = whole[ab * q : (ab + 1) * q]
        mid_ref[(3 * ab) * q : (3 * ab + 1) * q, :] = block[:, :mid]
        mid_ref[(3 * ab + 1) * q : (3 * ab + 2) * q, :] = block[:, mid:]
    half_rows = rows // 2
    last = whole[rows : rows + half_rows]
    last = jnp.concatenate([last[:, :mid], last[:, mid:]], axis=0)
    for ab in range(9):
        mid_ref[(3 * ab + 2) * q : (3 * ab + 3) * q, :] = last[ab * q : (ab + 1) * q]


def partner(block, bit):
    size = lax.axis_size("spatial")
    return lax.ppermute(block, "spatial", [(i, i ^ bit) for i in range(size)])


def across(block):
    size = lax.axis_size("spatial")
    pairs = [(i, i + 1) for i in range(1, size - 1, 2)]
    return lax.ppermute(block, "spatial", pairs + [(j, i) for i, j in pairs])


def bit_is_clear(bit):
    return (lax.axis_index("spatial") & bit) == 0


def rounded(block):
    return lax.optimization_barrier(block.astype(BF16))


def add_both(sent, bit):
    return sent.astype(F32) + partner(sent, bit).astype(F32)


def halves(block, low):
    rows = block.shape[0] // 2
    mine = jnp.where(low, block[:rows], block[rows:])
    other = jnp.where(low, block[rows:], block[:rows])
    return mine, rounded(other)


def in_order(block, other, low):
    return jnp.where(low, block, other), jnp.where(low, other, block)


def far_bits():
    return [1 << k for k in range(2, lax.axis_size("spatial").bit_length() - 1)]


def shards(volume, weights_mid, weights_top, cotangent):
    spatial = lax.axis_size("spatial")
    cin, nz, h, w = volume.shape
    mid = weights_mid.shape[0]
    cout, nzp, hp, wp = cotangent.shape
    shape = jax.ShapeDtypeStruct
    plane = h * w
    volume, first_core, low = lax.optimization_barrier((volume, bit_is_clear(1), bit_is_clear(4)))
    flat = volume.reshape(cin, nz * plane)
    early, late = flat[:, : (nz - 1) * plane], flat[:, plane:]
    far = across(jnp.where(first_core, early, late))
    near = partner(jnp.where(first_core, late, early), 1)
    split = weights_mid.reshape(mid, 9, 3, cin)
    wmid = jnp.transpose(split, (2, 0, 1, 3)).reshape(3 * mid, 9 * cin)
    wback = jnp.transpose(split, (2, 3, 1, 0)).reshape(3 * cin, 9 * mid)
    wtop = jnp.transpose(weights_top, (1, 2, 0)).reshape(27 * mid, cout)
    cot = cotangent.reshape(cout, nzp * hp * wp)
    size = (h + 2) * w
    count = nz // 2 + 2
    halo = nz - 1
    pool_size = (hp + 2) * wp
    vol_near, pre_near, pool_near = kernel_call(
        lambda *refs: near_kernel(*refs, h=h, w=w, spatial=spatial),
        "near_side",
        (
            shape((cin, (nz + halo) * size), BF16),
            shape((mid, count * plane), F32),
            shape((3 * mid, count // 2 * pool_size), BF16),
        ),
        (near, flat, wmid),
        flops=900_000_000,
        moved=3_000_000,
    )
    far, wback, vol_near, pool_near = lax.optimization_barrier((far, wback, vol_near, pool_near))
    top_rows = 27 * mid
    delta_rows = cot.size // cout
    delta, pre_far, vol, keep, send = kernel_call(
        lambda *refs: far_kernel(*refs, h=h, w=w, spatial=spatial),
        "far_side",
        (
            shape(cot.shape, BF16),
            shape((mid, count * plane), F32),
            shape((cin, (nz + 2 * halo) * size), BF16),
            shape((top_rows // 2, cout), F32),
            shape((delta_rows + top_rows // 2, cout), BF16),
        ),
        (far, vol_near, pool_near, wmid, wtop, cot),
        scratch=(pltpu.VMEM((3 * mid, count * pool_size), BF16), pltpu.VMEM((top_rows, cout), F32)),
        flops=1_100_000_000,
        moved=5_000_000,
    )
    delta_far = across(delta)
    slope = kernel_call(
        lambda *refs: slope_kernel(*refs, plane=plane),
        "slope",
        shape((mid, (nz + 2) * plane), F32),
        (pre_near, pre_far),
        flops=100_000_000,
        moved=3_000_000,
    )
    delta_near = partner(send, 1)
    mine, other = halves(keep + delta_near[delta_rows:].astype(F32), low)
    top_received = partner(other, 4)
    mid_rows = -(-27 * cin // 64) * 16
    side_scratch = (
        pltpu.VMEM((cout, 2 * nzp * (hp + 2) * wp), BF16),
        pltpu.VMEM((3 * mid, (nz // 2 + 1) * plane), BF16),
    )
    part, field_near = kernel_call(
        lambda *refs: backward_near_kernel(*refs, h=h, w=w, spatial=spatial),
        "backward_near",
        (shape((9 * cin, 3 * mid), F32), shape((mid, (nz // 2 + 1) * size), BF16)),
        (delta_near, delta, slope, vol, wtop),
        scratch=side_scratch,
        flops=500_000_000,
        moved=3_000_000,
    )
    delta_far, part, field_near = lax.optimization_barrier((delta_far, part, field_near))
    keep, send, field = kernel_call(
        lambda *refs: backward_far_kernel(*refs, h=h, w=w, spatial=spatial),
        "backward_far",
        (
            shape((mid_rows, 2 * mid), F32),
            shape((mid_rows, 2 * mid), BF16),
            shape((mid, (nz + 2) * size), BF16),
        ),
        (delta_far, delta, slope, vol, wtop, part, field_near),
        scratch=side_scratch + (pltpu.VMEM((2 * mid_rows, 2 * mid), F32),),
        flops=500_000_000,
        moved=4_000_000,
    )
    keep, send, mine, top_received = lax.optimization_barrier((keep, send, mine, top_received))
    top_sum = rounded(mine + top_received.astype(F32))
    bits = far_bits()[1:]
    top_sum, send = lax.optimization_barrier((top_sum, send))
    for bit in bits:
        top_sum = rounded(add_both(top_sum, bit))
    mid_sum = rounded(keep + partner(send, 1).astype(F32))
    mid_sum = rounded(add_both(mid_sum, 2))
    top_sum, _ = lax.optimization_barrier((top_sum, mid_sum))
    mid_sum = rounded(add_both(mid_sum, 4))
    mid_sum, field = lax.optimization_barrier((mid_sum, field))
    for bit in bits[:-1]:
        mid_sum = rounded(add_both(mid_sum, bit))
    mid_sum = add_both(mid_sum, bits[-1])
    top_sum = rounded(add_both(top_sum, 2))
    input_grad = kernel_call(
        lambda *refs: input_kernel(*refs, h=h, w=w),
        "input_grad",
        shape((cin, nz * plane), BF16),
        (field, wback),
        flops=452_000_000,
        moved=2_000_000,
    )
    top_sum, input_grad = lax.optimization_barrier((top_sum, input_grad))
    top_sum = jnp.concatenate(in_order(top_sum, partner(top_sum, 4), low), axis=0)
    mid_high = rounded(mid_sum)
    mid_low = rounded(mid_sum - mid_high.astype(F32))
    both = jnp.concatenate([top_sum, mid_high, mid_low], axis=0)
    top_grad, mid_grad = kernel_call(
        lambda *refs: finish_kernel(
            *refs,
            scale_top=1.0 / math.sqrt(nzp * hp * wp * spatial),
            scale_mid=1.0 / math.sqrt(nz * plane * spatial),
        ),
        "finish",
        (shape((27 * mid, cout), F32), shape((27 * cin, mid), F32)),
        (both, partner(both, 1)),
        moved=2_000_000,
        last=True,
    )
    return (
        input_grad.reshape(volume.shape),
        jnp.transpose(mid_grad.reshape(27, cin, mid), (2, 0, 1)),
        jnp.transpose(top_grad.reshape(27, mid, cout), (2, 0, 1)),
    )


def solution(mesh):
    return jax.shard_map(
        shards,
        mesh=mesh,
        in_specs=(P(None, "spatial", "groups", None), P(), P(), P(None, "spatial", "groups", None)),
        out_specs=(
            P(None, "spatial", "groups", None),
            P("groups", None, None),
            P("groups", None, None),
        ),
        check_vma=False,
    )
```

```python
import math

import jax
import jax.numpy as jnp
from jax import lax
from jax.experimental import pallas as pl
from jax.experimental.pallas import tpu as pltpu
from jax.sharding import PartitionSpec as P

BF16 = jnp.bfloat16
F32 = jnp.float32
ROOT = math.sqrt(2.0 / math.pi)
CUBIC = 0.044715
THREE = (0, 1, 2)
VMEM_LIMIT = 20 << 20


def kernel_call(body, name, outs, args, scratch=(), flops=0, moved=0, last=False):
    whole = pl.BlockSpec(memory_space=pltpu.VMEM)
    args = [pltpu.with_memory_space_constraint(arg, pltpu.VMEM) for arg in args]
    if not last:
        outs = jax.tree.map(lambda out: pltpu.VMEM(out.shape, out.dtype), outs)
    return pl.pallas_call(
        body,
        name=name,
        out_shape=outs,
        in_specs=[whole] * len(args),
        out_specs=jax.tree.map(lambda _: whole, outs),
        scratch_shapes=list(scratch),
        compiler_params=pltpu.CompilerParams(vmem_limit_bytes=VMEM_LIMIT),
        cost_estimate=pl.CostEstimate(flops=flops, bytes_accessed=moved, transcendentals=0),
    )(*args)


def dot(a, b, contract=((1,), (0,))):
    return lax.dot_general(a, b, (contract, ((), ())), preferred_element_type=F32)


def parity_matrix(width, inverse):
    first = lax.broadcasted_iota(jnp.int32, (width, width), 0)
    second = lax.broadcasted_iota(jnp.int32, (width, width), 1)
    cell, slot = (second, first) if inverse else (first, second)
    half = width // 2
    source = jnp.where(slot < half, 2 * slot, 2 * (slot - half) + 1)
    return (cell == source).astype(F32).astype(BF16)


def later(row):
    lane = lax.broadcasted_iota(jnp.int32, row.shape, 1)
    return jnp.where(lane == 0, 0.0, pltpu.roll(row, 1, 1))


def earlier(row):
    lane = lax.broadcasted_iota(jnp.int32, row.shape, 1)
    last = row.shape[1] - 1
    return jnp.where(lane == last, 0.0, pltpu.roll(row, last, 1))


def gelu(value):
    return (0.5 * value) * (1.0 + jnp.tanh(value * (ROOT + ROOT * CUBIC * (value * value))))


def gelu_slope(value):
    square = value * value
    tanh = jnp.tanh(value * (ROOT + ROOT * CUBIC * square))
    inner = 0.5 * ROOT + 1.5 * ROOT * CUBIC * square
    return 0.5 + 0.5 * tanh + value * inner * (1.0 - tanh * tanh)


def sort_plane(rows, split, store, h, w):
    channels = rows[0].shape[0]
    done = dot(jnp.concatenate(rows, axis=0), split).astype(BF16)
    store(0, jnp.zeros((channels, w), BF16))
    store(h + 1, jnp.zeros((channels, w), BF16))
    for y in range(h):
        store(y + 1, done[y * channels : (y + 1) * channels])


def lanes(start, size):
    return pl.ds(pl.multiple_of(start, 128), size)


def middle_planes(vol_ref, wmid_ref, pre_ref, begin, count, h, w, emit):
    half = w // 2
    mid = pre_ref.shape[0]
    for pz in range(count // 2):
        sums = [None] * (h // 2)
        for j in (2 * pz, 2 * pz + 1):
            at = (begin + j) * (h + 2) * w
            cols = jnp.concatenate([vol_ref[:, lanes(at + (a * (h + 2) + b) * w, h * w)] for a in THREE for b in THREE], axis=0)
            part = dot(wmid_ref[...], cols)
            for y in range(h):
                even = slice(y * w, y * w + half)
                odd = slice(y * w + half, (y + 1) * w)
                pre_even = part[mid : 2 * mid, even] + later(part[:mid, odd]) + part[2 * mid :, odd]
                pre_odd = part[mid : 2 * mid, odd] + part[:mid, even] + earlier(part[2 * mid :, even])
                out = (j * h + y) * w
                pre_ref[:, out : out + half] = pre_even
                pre_ref[:, out + half : out + w] = pre_odd
                both = gelu(pre_even) + gelu(pre_odd)
                sums[y // 2] = both if sums[y // 2] is None else sums[y // 2] + both
        emit(pz, [row * 0.125 for row in sums])


def pool_rows(pool_ref, base, rows, outside):
    mid, half = rows[0].shape
    zero = jnp.zeros((3 * mid, half), BF16)
    pool_ref[:, lanes(base, half)] = zero
    pool_ref[:, lanes(base + (len(rows) + 1) * half, half)] = zero
    for y, row in enumerate(rows):
        row = jnp.where(outside, 0.0, row).astype(BF16)
        wide = row.astype(F32)
        at = lanes(base + (y + 1) * half, half)
        pool_ref[:mid, at] = later(wide).astype(BF16)
        pool_ref[mid : 2 * mid, at] = row
        pool_ref[2 * mid :, at] = earlier(wide).astype(BF16)


def near_kernel(near_ref, own_ref, wmid_ref, vol_ref, pre_ref, pool_ref, *, h, w, spatial):
    here = lax.axis_index("spatial")
    core = here % 2
    split = parity_matrix(w, False)
    size = (h + 2) * w
    halo = near_ref.shape[1] // (h * w)
    own = own_ref.shape[1] // (h * w)
    for ref, count, start in ((own_ref, own, core * halo), (near_ref, halo, (1 - core) * own)):
        for z in range(count):
            rows = [ref[:, (z * h + y) * w : (z * h + y + 1) * w] for y in range(h)]

            def store(row, value, at=(start + z) * size):
                vol_ref[:, lanes(at + row * w, w)] = value

            sort_plane(rows, split, store, h, w)
    count = pre_ref.shape[1] // (h * w)
    pooled = count // 2
    prow = pool_ref.shape[1] // pooled

    def emit(pz, rows):
        first = (core == 1) & (here == 0) if pz == 0 else False
        last = (core == 0) & (here == spatial - 1) if pz == pooled - 1 else False
        pool_rows(pool_ref, pz * prow, rows, jnp.logical_or(first, last))

    middle_planes(vol_ref, wmid_ref, pre_ref, 1 - core, count, h, w, emit)


def far_kernel(
    far_ref, vol_near_ref, pool_near_ref, wmid_ref, wtop_ref, cot_ref, delta_ref, pre_ref, vol_ref, keep_ref, send_ref, pool_ref,
    grad_ref, *, h, w, spatial
):
    half = w // 2
    here = lax.axis_index("spatial")
    core = here % 2
    split = parity_matrix(w, False)
    size = (h + 2) * w
    halo = far_ref.shape[1] // (h * w)
    known = vol_near_ref.shape[1]
    vol_ref[:, lanes((1 - core) * halo * size, known)] = vol_near_ref[...]
    for z in range(halo):
        rows = [far_ref[:, (z * h + y) * w : (z * h + y + 1) * w] for y in range(h)]

        def store(row, value, at=core * known + z * size):
            vol_ref[:, lanes(at + row * w, w)] = value

        sort_plane(rows, split, store, h, w)
    count = pre_ref.shape[1] // (h * w)
    pooled = count // 2
    hp = h // 2
    prow = (hp + 2) * half
    pool_ref[:, lanes((1 - core) * pooled * prow, pooled * prow)] = pool_near_ref[...]

    def emit(pz, rows):
        first = (core == 0) & (here == 0) if pz == 0 else False
        last = (core == 1) & (here == spatial - 1) if pz == pooled - 1 else False
        pool_rows(pool_ref, (core * pooled + pz) * prow, rows, jnp.logical_or(first, last))

    middle_planes(vol_ref, wmid_ref, pre_ref, core * count, count, h, w, emit)
    for j in range(delta_ref.shape[1] // (hp * half)):
        cols = jnp.concatenate(
            [pool_ref[:, (j + a) * prow + b * half : (j + a) * prow + (b + hp) * half] for a in THREE for b in THREE], axis=0
        )
        pre_top = dot(wtop_ref[...], cols, ((0,), (0,)))
        at = slice(j * hp * half, (j + 1) * hp * half)
        delta_ref[:, at] = (cot_ref[:, at].astype(F32) * gelu_slope(pre_top)).astype(BF16)
    top_part(delta_ref, pool_ref, keep_ref, send_ref, grad_ref, hp, half)


def halve(whole_ref, keep_ref, send_ref):
    core = lax.axis_index("spatial") % 2
    rows = keep_ref.shape[0]
    keep_ref[...] = whole_ref[pl.ds(pl.multiple_of(core * rows, 16), rows), :]
    sent = whole_ref[pl.ds(pl.multiple_of((1 - core) * rows, 16), rows), :].astype(BF16)
    send_ref[send_ref.shape[0] - rows :, :] = sent


def slope_kernel(near_ref, far_ref, slope_ref, *, plane):
    core = lax.axis_index("spatial") % 2
    part = slope_ref.shape[1] // 2
    for ref, side in ((near_ref, 1 - core), (far_ref, core)):
        for at in range(0, part, 128):
            value = 0.125 * gelu_slope(ref[:, lanes((1 - side) * plane + at, 128)])
            slope_ref[:, lanes(side * part + at, 128)] = value


def top_part(delta_ref, pool_ref, keep_ref, send_ref, out_ref, hp, wp):
    cout = delta_ref.shape[0]
    for at in range(0, delta_ref.shape[1], wp):
        send_ref[at // wp * cout : (at // wp + 1) * cout, :] = delta_ref[:, at : at + wp]
    prow = (hp + 2) * wp
    planes = delta_ref.shape[1] // (hp * wp)
    for a in THREE:
        for b in THREE:
            block = jnp.concatenate(
                [pool_ref[:, (j + a) * prow + b * wp : (j + a) * prow + (b + hp) * wp] for j in range(planes)], axis=1
            )
            rows = slice((3 * a + b) * block.shape[0], (3 * a + b + 1) * block.shape[0])
            out_ref[rows, :] = dot(block, delta_ref[...], ((1,), (1,)))
    halve(out_ref, keep_ref, send_ref)


def backward_side(side, neighbour, own_ref, slope_ref, vol_ref, wtop_ref, field_ref, field_base, top_ref, shift_ref, h, w, spatial):
    half, hp = w // 2, h // 2
    here = lax.axis_index("spatial")
    trow = (hp + 2) * half
    depth = own_ref.shape[1] // (hp * half)
    zero = jnp.zeros((top_ref.shape[0], half), BF16)
    for z in range(depth):
        near_plane = neighbour(z)
        own_plane = own_ref[:, z * hp * half : (z + 1) * hp * half]
        for plane, base in ((own_plane, (1 - side) * depth * trow), (near_plane, side * depth * trow)):
            base = base + z * trow
            top_ref[:, lanes(base, half)] = zero
            top_ref[:, lanes(base + half, hp * half)] = plane
            top_ref[:, lanes(base + (hp + 1) * half, half)] = zero
    mid = slope_ref.shape[0]
    weights = jnp.concatenate(
        [
            jnp.concatenate([wtop_ref[(3 * ab + c) * mid : (3 * ab + c + 1) * mid, :] for ab in range(9)], axis=1)
            for c in THREE
        ],
        axis=0,
    )
    count = 2 * depth - 2
    cols = jnp.concatenate(
        [
            jnp.concatenate(
                [
                    top_ref[:, (j + 2 - a) * trow + (2 - b) * half : (j + 2 - a) * trow + (2 - b + hp) * half]
                    for j in range(count)
                ],
                axis=1,
            )
            for a in THREE
            for b in THREE
        ],
        axis=0,
    )
    part = dot(weights, cols)
    pools = []
    for k in range(count * hp):
        at = slice(k * half, (k + 1) * half)
        pools.append(part[mid : 2 * mid, at] + later(part[2 * mid :, at]) + earlier(part[:mid, at]))
    size = (h + 2) * w
    field_zero = jnp.zeros((mid, w), BF16)
    planes = 2 * count - 1
    for k in range(planes):
        base = field_base + k * size
        field_ref[:, lanes(base, w)] = field_zero
        field_ref[:, lanes(base + (h + 1) * w, w)] = field_zero
        for y in range(h):
            pool = jnp.where(side == 1, pools[k // 2 * hp + y // 2], pools[(k + 1) // 2 * hp + y // 2])
            if k == 0:
                pool = jnp.where((side == 0) & (here == 0), 0.0, pool)
            if k == planes - 1:
                pool = jnp.where((side == 1) & (here == spatial - 1), 0.0, pool)
            row = (k * h + y) * w
            at = side * planes * h * w + row
            even = (slope_ref[:, lanes(at, half)] * pool).astype(BF16)
            odd = (slope_ref[:, lanes(at + half, half)] * pool).astype(BF16)
            to = base + (y + 1) * w
            field_ref[:, lanes(to, half)] = even
            field_ref[:, lanes(to + half, half)] = odd
            shift_ref[:mid, row : row + half] = odd
            shift_ref[:mid, row + half : row + w] = earlier(even.astype(F32)).astype(BF16)
            shift_ref[mid : 2 * mid, row : row + half] = even
            shift_ref[mid : 2 * mid, row + half : row + w] = odd
            shift_ref[2 * mid :, row : row + half] = later(odd.astype(F32)).astype(BF16)
            shift_ref[2 * mid :, row + half : row + w] = even
    total = None
    for z in range(depth):
        at = (side * depth + z + 2) * size
        piece = jnp.concatenate([vol_ref[:, lanes(at + a * size + b * w, h * w)] for a in THREE for b in THREE], axis=0)
        moved = shift_ref[:, lanes((1 - side + z) * h * w, h * w)]
        product = dot(piece, moved, ((1,), (1,)))
        total = product if total is None else total + product
    return total


def backward_near_kernel(
    near_ref, own_ref, slope_ref, vol_ref, wtop_ref, part_ref, field_ref, top_ref, shift_ref, *, h, w, spatial
):
    core = lax.axis_index("spatial") % 2
    hp = h // 2
    cout = own_ref.shape[0]

    def neighbour(z):
        return jnp.concatenate([near_ref[k * cout : (k + 1) * cout, :] for k in range(z * hp, (z + 1) * hp)], axis=1)

    part_ref[...] = backward_side(
        1 - core, neighbour, own_ref, slope_ref, vol_ref, wtop_ref, field_ref, 0, top_ref, shift_ref, h, w, spatial
    )


def backward_far_kernel(
    far_ref, own_ref, slope_ref, vol_ref, wtop_ref, part_ref, field_near_ref, keep_ref, send_ref, field_ref, top_ref, shift_ref,
    mid_ref, *, h, w, spatial
):
    core = lax.axis_index("spatial") % 2
    size = h // 2 * (w // 2)
    known = field_near_ref.shape[1]
    field_ref[:, lanes((1 - core) * known, known)] = field_near_ref[...]

    def neighbour(z):
        return far_ref[:, z * size : (z + 1) * size]

    total = part_ref[...] + backward_side(
        core, neighbour, own_ref, slope_ref, vol_ref, wtop_ref, field_ref, core * known, top_ref, shift_ref, h, w, spatial
    )
    mid = field_ref.shape[0]
    rows = total.shape[0]
    half_rows = rows // 2
    mid_ref[:rows, :] = total[:, : 2 * mid]
    last = total[:, 2 * mid :]
    mid_ref[rows : rows + half_rows, :] = jnp.concatenate([last[:half_rows], last[half_rows:]], axis=1)
    spare = mid_ref.shape[0] - rows - half_rows
    if spare:
        mid_ref[rows + half_rows :, :] = jnp.zeros((spare, 2 * mid), F32)
    halve(mid_ref, keep_ref, send_ref)


def input_kernel(field_ref, wback_ref, out_ref, *, h, w):
    half = w // 2
    vrows = h + 2
    join = parity_matrix(w, True)
    ch = out_ref.shape[0]
    for z in range(out_ref.shape[1] // (h * w)):
        cols = jnp.concatenate(
            [
                field_ref[:, ((z + 2 - a) * vrows + 2 - b) * w : ((z + 2 - a) * vrows + 2 - b + h) * w]
                for a in THREE
                for b in THREE
            ],
            axis=0,
        )
        part = dot(wback_ref[...], cols)
        rows = []
        for y in range(h):
            even = slice(y * w, y * w + half)
            odd = slice(y * w + half, (y + 1) * w)
            grad_even = part[ch : 2 * ch, even] + later(part[2 * ch :, odd]) + part[:ch, odd]
            grad_odd = part[ch : 2 * ch, odd] + part[2 * ch :, even] + earlier(part[:ch, even])
            rows.append(jnp.concatenate([grad_even, grad_odd], axis=1).astype(BF16))
        joined = dot(jnp.concatenate(rows, axis=0), join).astype(BF16)
        for y in range(h):
            out_ref[:, (z * h + y) * w : (z * h + y + 1) * w] = joined[y * ch : (y + 1) * ch]


def finish_kernel(own_ref, other_ref, top_ref, mid_ref, *, scale_top, scale_mid):
    core = lax.axis_index("spatial") % 2
    top_rows = top_ref.shape[0] // 2
    top_ref[pl.ds(pl.multiple_of(core * top_rows, 16), top_rows), :] = own_ref[:top_rows].astype(F32) * scale_top
    top_ref[pl.ds(pl.multiple_of((1 - core) * top_rows, 16), top_rows), :] = other_ref[:top_rows].astype(F32) * scale_top
    mid_rows = (own_ref.shape[0] - top_rows) // 2
    own = own_ref[top_rows : top_rows + mid_rows].astype(F32) + own_ref[top_rows + mid_rows :].astype(F32)
    other = other_ref[top_rows : top_rows + mid_rows].astype(F32) + other_ref[top_rows + mid_rows :].astype(F32)
    low = jnp.where(core == 0, own, other)
    high = jnp.where(core == 0, other, own)
    whole = jnp.concatenate([low, high], axis=0) * scale_mid
    rows = mid_ref.shape[0] // 3
    mid = mid_ref.shape[1]
    q = rows // 9
    for ab in range(9):
        block = whole[ab * q : (ab + 1) * q]
        mid_ref[(3 * ab) * q : (3 * ab + 1) * q, :] = block[:, :mid]
        mid_ref[(3 * ab + 1) * q : (3 * ab + 2) * q, :] = block[:, mid:]
    half_rows = rows // 2
    last = whole[rows : rows + half_rows]
    last = jnp.concatenate([last[:, :mid], last[:, mid:]], axis=0)
    for ab in range(9):
        mid_ref[(3 * ab + 2) * q : (3 * ab + 3) * q, :] = last[ab * q : (ab + 1) * q]


def partner(block, bit):
    size = lax.axis_size("spatial")
    return lax.ppermute(block, "spatial", [(i, i ^ bit) for i in range(size)])


def across(block):
    size = lax.axis_size("spatial")
    pairs = [(i, i + 1) for i in range(1, size - 1, 2)]
    return lax.ppermute(block, "spatial", pairs + [(j, i) for i, j in pairs])


def bit_is_clear(bit):
    return (lax.axis_index("spatial") & bit) == 0


def rounded(block):
    return lax.optimization_barrier(block.astype(BF16))


def add_both(sent, bit):
    return sent.astype(F32) + partner(sent, bit).astype(F32)


def halves(block, low):
    rows = block.shape[0] // 2
    mine = jnp.where(low, block[:rows], block[rows:])
    other = jnp.where(low, block[rows:], block[:rows])
    return mine, rounded(other)


def in_order(block, other, low):
    return jnp.where(low, block, other), jnp.where(low, other, block)


def far_bits():
    return [1 << k for k in range(2, lax.axis_size("spatial").bit_length() - 1)]


def shards(volume, weights_mid, weights_top, cotangent):
    spatial = lax.axis_size("spatial")
    cin, nz, h, w = volume.shape
    mid = weights_mid.shape[0]
    cout, nzp, hp, wp = cotangent.shape
    shape = jax.ShapeDtypeStruct
    plane = h * w
    volume, first_core, low = lax.optimization_barrier((volume, bit_is_clear(1), bit_is_clear(4)))
    flat = volume.reshape(cin, nz * plane)
    early, late = flat[:, : (nz - 1) * plane], flat[:, plane:]
    far = across(jnp.where(first_core, early, late))
    near = partner(jnp.where(first_core, late, early), 1)
    split = weights_mid.reshape(mid, 9, 3, cin)
    wmid = jnp.transpose(split, (2, 0, 1, 3)).reshape(3 * mid, 9 * cin)
    wback = jnp.transpose(split, (2, 3, 1, 0)).reshape(3 * cin, 9 * mid)
    wtop = jnp.transpose(weights_top, (1, 2, 0)).reshape(27 * mid, cout)
    cot = cotangent.reshape(cout, nzp * hp * wp)
    size = (h + 2) * w
    count = nz // 2 + 2
    halo = nz - 1
    pool_size = (hp + 2) * wp
    vol_near, pre_near, pool_near = kernel_call(
        lambda *refs: near_kernel(*refs, h=h, w=w, spatial=spatial),
        "near_side",
        (
            shape((cin, (nz + halo) * size), BF16),
            shape((mid, count * plane), F32),
            shape((3 * mid, count // 2 * pool_size), BF16),
        ),
        (near, flat, wmid),
        flops=900_000_000,
        moved=3_000_000,
    )
    far, wback, vol_near, pool_near = lax.optimization_barrier((far, wback, vol_near, pool_near))
    top_rows = 27 * mid
    delta_rows = cot.size // cout
    delta, pre_far, vol, keep, send = kernel_call(
        lambda *refs: far_kernel(*refs, h=h, w=w, spatial=spatial),
        "far_side",
        (
            shape(cot.shape, BF16),
            shape((mid, count * plane), F32),
            shape((cin, (nz + 2 * halo) * size), BF16),
            shape((top_rows // 2, cout), F32),
            shape((delta_rows + top_rows // 2, cout), BF16),
        ),
        (far, vol_near, pool_near, wmid, wtop, cot),
        scratch=(pltpu.VMEM((3 * mid, count * pool_size), BF16), pltpu.VMEM((top_rows, cout), F32)),
        flops=1_100_000_000,
        moved=5_000_000,
    )
    delta_far = across(delta)
    slope = kernel_call(
        lambda *refs: slope_kernel(*refs, plane=plane),
        "slope",
        shape((mid, (nz + 2) * plane), F32),
        (pre_near, pre_far),
        flops=100_000_000,
        moved=3_000_000,
    )
    delta_near = partner(send, 1)
    mine, other = halves(keep + delta_near[delta_rows:].astype(F32), low)
    top_received = partner(other, 4)
    mid_rows = -(-27 * cin // 64) * 16
    side_scratch = (
        pltpu.VMEM((cout, 2 * nzp * (hp + 2) * wp), BF16),
        pltpu.VMEM((3 * mid, (nz // 2 + 1) * plane), BF16),
    )
    part, field_near = kernel_call(
        lambda *refs: backward_near_kernel(*refs, h=h, w=w, spatial=spatial),
        "backward_near",
        (shape((9 * cin, 3 * mid), F32), shape((mid, (nz // 2 + 1) * size), BF16)),
        (delta_near, delta, slope, vol, wtop),
        scratch=side_scratch,
        flops=500_000_000,
        moved=3_000_000,
    )
    delta_far, part, field_near = lax.optimization_barrier((delta_far, part, field_near))
    keep, send, field = kernel_call(
        lambda *refs: backward_far_kernel(*refs, h=h, w=w, spatial=spatial),
        "backward_far",
        (
            shape((mid_rows, 2 * mid), F32),
            shape((mid_rows, 2 * mid), BF16),
            shape((mid, (nz + 2) * size), BF16),
        ),
        (delta_far, delta, slope, vol, wtop, part, field_near),
        scratch=side_scratch + (pltpu.VMEM((2 * mid_rows, 2 * mid), F32),),
        flops=500_000_000,
        moved=4_000_000,
    )
    keep, send, mine, top_received = lax.optimization_barrier((keep, send, mine, top_received))
    top_sum = rounded(mine + top_received.astype(F32))
    bits = far_bits()[1:]
    top_sum, send = lax.optimization_barrier((top_sum, send))
    for bit in bits:
        top_sum = rounded(add_both(top_sum, bit))
    mid_sum = rounded(keep + partner(send, 1).astype(F32))
    mid_sum = rounded(add_both(mid_sum, 4))
    mid_sum = rounded(add_both(mid_sum, 2))
    mid_sum, field = lax.optimization_barrier((mid_sum, field))
    for bit in bits[:-1]:
        mid_sum = rounded(add_both(mid_sum, bit))
    mid_sum = add_both(mid_sum, bits[-1])
    top_sum = rounded(add_both(top_sum, 2))
    input_grad = kernel_call(
        lambda *refs: input_kernel(*refs, h=h, w=w),
        "input_grad",
        shape((cin, nz * plane), BF16),
        (field, wback),
        flops=452_000_000,
        moved=2_000_000,
    )
    top_sum, input_grad = lax.optimization_barrier((top_sum, input_grad))
    top_sum = jnp.concatenate(in_order(top_sum, partner(top_sum, 4), low), axis=0)
    mid_high = rounded(mid_sum)
    mid_low = rounded(mid_sum - mid_high.astype(F32))
    both = jnp.concatenate([top_sum, mid_high, mid_low], axis=0)
    top_grad, mid_grad = kernel_call(
        lambda *refs: finish_kernel(
            *refs,
            scale_top=1.0 / math.sqrt(nzp * hp * wp * spatial),
            scale_mid=1.0 / math.sqrt(nz * plane * spatial),
        ),
        "finish",
        (shape((27 * mid, cout), F32), shape((27 * cin, mid), F32)),
        (both, partner(both, 1)),
        moved=2_000_000,
        last=True,
    )
    return (
        input_grad.reshape(volume.shape),
        jnp.transpose(mid_grad.reshape(27, cin, mid), (2, 0, 1)),
        jnp.transpose(top_grad.reshape(27, mid, cout), (2, 0, 1)),
    )


def solution(mesh):
    return jax.shard_map(
        shards,
        mesh=mesh,
        in_specs=(P(None, "spatial", "groups", None), P(), P(), P(None, "spatial", "groups", None)),
        out_specs=(
            P(None, "spatial", "groups", None),
            P("groups", None, None),
            P("groups", None, None),
        ),
        check_vma=False,
    )
```
